256 devices in a mesh: feat: 16 (over x_lo, z), dp: 16 (over y, x_hi, core).
Axes of the slice: x: 4 (x_hi: 2, x_lo: 2; x = x_hi * 2 + x_lo), y: 4, z: 8, core: 2. Of those that a mesh axis runs over, the one named last changes fastest.
Arguments:
- node_feats: bfloat16 [16, 6144, 1024], P('dp', None, 'feat'), may hold values from -6 to 6
- target_ids: int32 [16, 1536], P('dp'), may hold values from 0 to 6143
- layer_one_nbrs: int32 [16, 1536, 10], P('dp'), may hold values from 0 to 6143
- layer_one_counts: int32 [16, 1536], P('dp'), may hold values from 1 to 10
- layer_two_nbrs: int32 [16, 256, 5], P('dp', 'feat'), may hold values from 0 to 95
- layer_two_counts: int32 [16, 256], P('dp', 'feat'), may hold values from 1 to 5
- labels: int32 [16, 256], P('dp', 'feat'), may hold values from 0 to 18
- layer_one_weight: bfloat16 [2, 1024, 1024], P(None, 'feat'), may hold values from -0.1875 to 0.1875
- layer_two_weight: bfloat16 [2, 1024, 1024], replicated, may hold values from -0.1875 to 0.1875
- head_weight: bfloat16 [1024, 19], replicated, may hold values from -0.1875 to 0.1875
Outputs:
- hidden: bfloat16 [16, 1536, 1024], P('dp', 'feat')
- logits: float32 [16, 256, 19], P('dp', 'feat')
- grad_one: float32 [2, 1024, 1024], P(None, 'feat', 'dp')
- grad_two: float32 [2, 1024, 1024], P(None, 'feat', 'dp')
- grad_head: float32 [1024, 19], P('feat')
The draws below stay inside these ranges and needn't reach their ends.
Inputs may be any that keep to these rules, and one draw needn't show every extreme that they name: `target_ids`: rows of the micro-batch's sampled nodes. `layer_one_nbrs`: slots past a row's count are padding and are ignored. `layer_two_nbrs`: rows of the seed owner's block of 96 layer-one rows; slots past the seed's count are padding and are ignored.
All inputs are finite; a program needn't handle non-finite values.
Results may differ from the reference program's by a relative error of at most 0.03.
Values may be sent and summed in bfloat16 or wider, within the bound.
A program may use at most 128 MiB of HBM per device.

```python
import jax
import jax.numpy as jnp
from jax import lax

F = 1024
H = 1024
C = 19
FAN1 = 10
FAN2 = 5
SEED_DEV = 16
HROWS = 96
TARGETS = 1536
SEEDS = 256
NODES = 6144
COLS_DEV = 64
N_FEAT = 16
N_DP = 16


def with_ends(result, key, low, largest):
    longest = result.shape.index(max(result.shape))
    spots = []
    for shift in (0, 1):
        where = [jax.random.randint(jax.random.fold_in(key, axis), (), 0, length) for axis, length in enumerate(result.shape)]
        where[longest] = (where[longest] + shift) % result.shape[longest]
        spots.append(tuple(where))
    return result.at[spots[0]].set(low).at[spots[1]].set(largest)


def shard_levels(key, shape, shards, least, top_value):
    def one(axis_at, parts):
        steps = jax.random.uniform(jax.random.fold_in(jax.random.fold_in(key, 6), axis_at), (parts,), jnp.float32, least / len(shards), top_value / len(shards))
        return jnp.repeat(jnp.exp(steps), shape[axis_at] // parts).reshape((-1,) + (1,) * (len(shape) - axis_at - 1))

    loudness = one(*shards[0])
    for cut in shards[1:]:
        loudness = loudness * one(*cut)
    return loudness


def normal_values(rng, shape, scale, most, shards=(), kind=jnp.bfloat16):
    drawn = scale * jax.random.normal(rng, shape, jnp.float32)
    if shards:
        drawn = drawn * shard_levels(rng, shape, shards, -0.22, 0.18)
    return jnp.clip(drawn, -most, most).astype(kind)


def setup_inputs(seed: int = 0) -> dict:
    seeds = jax.random.split(jax.random.key(seed), 11)
    node_feats = normal_values(seeds[0], (N_DP, NODES, F), 1.0, 6.0, ((0, 16), (2, 16)))
    target_ids = with_ends(jax.random.randint(seeds[1], (N_DP, TARGETS), 0, NODES), jax.random.fold_in(seeds[1], 1), 0, NODES - 1).astype(jnp.int32)
    layer_one_nbrs = with_ends(jax.random.randint(seeds[2], (N_DP, TARGETS, FAN1), 0, NODES), jax.random.fold_in(seeds[2], 1), 0, NODES - 1).astype(jnp.int32)
    layer_one_counts = with_ends(jax.random.randint(seeds[3], (N_DP, TARGETS), 1, FAN1 + 1), jax.random.fold_in(seeds[3], 1), 1, FAN1).astype(jnp.int32)
    layer_two_nbrs = with_ends(jax.random.randint(seeds[4], (N_DP, SEEDS, FAN2), 0, HROWS), jax.random.fold_in(seeds[4], 1), 0, HROWS - 1).astype(jnp.int32)
    layer_two_counts = with_ends(jax.random.randint(seeds[5], (N_DP, SEEDS), 1, FAN2 + 1), jax.random.fold_in(seeds[5], 1), 1, FAN2).astype(jnp.int32)
    labels = with_ends(jax.random.randint(seeds[6], (N_DP, SEEDS), 0, C), jax.random.fold_in(seeds[6], 1), 0, C - 1).astype(jnp.int32)
    layer_one_weight = normal_values(seeds[7], (2, F, H), F ** -0.5, 0.1875, ((1, 16),))
    layer_two_weight = normal_values(seeds[8], (2, H, H), H ** -0.5, 0.1875)
    head_weight = normal_values(seeds[9], (H, C), H ** -0.5, 0.1875)
    return dict(node_feats=node_feats, target_ids=target_ids, layer_one_nbrs=layer_one_nbrs, layer_one_counts=layer_one_counts, layer_two_nbrs=layer_two_nbrs, layer_two_counts=layer_two_counts, labels=labels, layer_one_weight=layer_one_weight, layer_two_weight=layer_two_weight, head_weight=head_weight)


def silu_slope(values):
    sigma = jax.nn.sigmoid(values)
    return sigma + values * sigma * (1.0 - sigma)


def owner_step(hidden_rows, pre_rows, neighbours, counts, targets, two_weight, head_weight):
    seed_hidden = hidden_rows[:SEED_DEV]
    valid = jnp.arange(FAN2)[None, :] < counts[:, None]
    count_float = counts.astype(jnp.float32)
    picked = jnp.take(hidden_rows, neighbours, axis=0).astype(jnp.float32)
    neigh_mean = (jnp.sum(jnp.where(valid[:, :, None], picked, 0.0), axis=1) / count_float[:, None]).astype(jnp.bfloat16)
    upper_pre = jnp.dot(seed_hidden, two_weight[0], preferred_element_type=jnp.float32) + jnp.dot(neigh_mean, two_weight[1], preferred_element_type=jnp.float32)
    upper_hidden = jax.nn.silu(upper_pre).astype(jnp.bfloat16)
    logits = jnp.dot(upper_hidden, head_weight, preferred_element_type=jnp.float32)
    probability = jax.nn.softmax(logits, axis=-1)
    one_hot = (targets[:, None] == jnp.arange(C)[None, :]).astype(jnp.float32)
    grad_logits = ((probability - one_hot) / SEEDS).astype(jnp.bfloat16)
    grad_head = jnp.dot(upper_hidden.T, grad_logits, preferred_element_type=jnp.float32)
    back_hidden = jnp.dot(grad_logits, head_weight.T, preferred_element_type=jnp.float32)
    grad_upper = (back_hidden * silu_slope(upper_pre)).astype(jnp.bfloat16)
    grad_self = jnp.dot(seed_hidden.T, grad_upper, preferred_element_type=jnp.float32)
    grad_neigh = jnp.dot(neigh_mean.T, grad_upper, preferred_element_type=jnp.float32)
    back_seed = jnp.dot(grad_upper, two_weight[0].T, preferred_element_type=jnp.float32)
    back_mean = jnp.dot(grad_upper, two_weight[1].T, preferred_element_type=jnp.float32)
    slot_weight = jnp.where(valid, 1.0 / count_float[:, None], 0.0)
    back_rows = jnp.zeros((HROWS, H), jnp.float32).at[:SEED_DEV].add(back_seed)
    spread = (back_mean[:, None, :] * slot_weight[:, :, None]).reshape(SEED_DEV * FAN2, H)
    back_rows = back_rows.at[neighbours.reshape(SEED_DEV * FAN2)].add(spread)
    grad_pre = (back_rows * silu_slope(pre_rows)).astype(jnp.bfloat16)
    return logits, grad_head, jnp.stack([grad_self, grad_neigh]), grad_pre


def group_step(group_items, one_weight, two_weight, head_weight):
    features, targets_in, one_nbrs, one_counts, two_nbrs, two_counts, seed_labels = group_items
    self_rows = jnp.take(features, targets_in, axis=0)
    valid = jnp.arange(FAN1)[None, :] < one_counts[:, None]
    picked = jnp.take(features, one_nbrs, axis=0).astype(jnp.float32)
    mean_rows = (jnp.sum(jnp.where(valid[:, :, None], picked, 0.0), axis=1) / one_counts[:, None].astype(jnp.float32)).astype(jnp.bfloat16)
    pre_act = jnp.zeros((TARGETS, H), jnp.float32)
    for block in range(N_FEAT):
        first = block * COLS_DEV
        block_term = jnp.dot(self_rows[:, first:first + COLS_DEV], one_weight[0, first:first + COLS_DEV], preferred_element_type=jnp.float32)
        block_term = block_term + jnp.dot(mean_rows[:, first:first + COLS_DEV], one_weight[1, first:first + COLS_DEV], preferred_element_type=jnp.float32)
        pre_act = pre_act + lax.optimization_barrier(block_term.astype(jnp.bfloat16)).astype(jnp.float32)
    hidden = jax.nn.silu(pre_act).astype(jnp.bfloat16)
    per_owner = jax.vmap(owner_step, in_axes=(0, 0, 0, 0, 0, None, None))
    logits, grad_head, grad_two, grad_pre = per_owner(
        hidden.reshape(N_FEAT, HROWS, H), pre_act.reshape(N_FEAT, HROWS, H),
        two_nbrs.reshape(N_FEAT, SEED_DEV, FAN2), two_counts.reshape(N_FEAT, SEED_DEV),
        seed_labels.reshape(N_FEAT, SEED_DEV), two_weight, head_weight)
    grad_pre = grad_pre.reshape(TARGETS, H)
    grad_one = jnp.stack([
        jnp.dot(self_rows.T, grad_pre, preferred_element_type=jnp.float32),
        jnp.dot(mean_rows.T, grad_pre, preferred_element_type=jnp.float32)])
    return hidden, logits.reshape(SEEDS, C), grad_one, jnp.sum(grad_two, axis=0), jnp.sum(grad_head, axis=0)


def reference(node_feats, target_ids, layer_one_nbrs, layer_one_counts, layer_two_nbrs, layer_two_counts, labels, layer_one_weight, layer_two_weight, head_weight):
    def run_group(group_items):
        return group_step(group_items, layer_one_weight, layer_two_weight, head_weight)

    hidden, logits, grad_one, grad_two, grad_head = lax.map(
        run_group, (node_feats, target_ids, layer_one_nbrs, layer_one_counts, layer_two_nbrs, layer_two_counts, labels))
    return hidden, logits, jnp.sum(grad_one, axis=0), jnp.sum(grad_two, axis=0), jnp.sum(grad_head, axis=0)
```

```python
import functools

import jax
import jax.numpy as jnp
from jax import lax
from jax.experimental import pallas as pl
from jax.experimental.pallas import tpu as pltpu
from jax.sharding import PartitionSpec as P

MESH = pl.DeviceIdType.MESH
BF16 = jnp.bfloat16
F32 = jnp.float32

NODES = 6144
ROWS = 96
SEEDS = 16
FAN1 = 10
FAN2 = 5
CLASSES = 19
WIDE = 1024
TN = (((0,), (0,)), ((), ()))
NT = (((1,), (1,)), ((), ()))


def sigmoid(values):
    return 1.0 / (1.0 + jnp.exp(-values))


def silu_slope(values):
    sigma = sigmoid(values)
    return sigma + values * sigma * (1.0 - sigma)


def kernel(
    idx_ref, inv_ref, feats_hbm, w1_hbm, w2_hbm, head_ref, nbr_ref, cnt_ref, lab_ref,
    hidden_ref, logits_ref, one_ref, two_ref, ghead_ref,
    feats, tab, rows, a4, a_full, w1, w2, headp, pre, p_send, p_recv, g_send, g_recv, z_send, z_recv, hd_send, hd_recv,
    load_sem, wa_s, wa_r, wb_s, wb_r, wc_s, wc_r, m1_s, m1_r, mq_s, mq_r, m2_s, m2_r, m3_s, m3_r, m4_s, m4_r, m5_s, m5_r,
):
    f = lax.axis_index("feat")
    d = lax.axis_index("dp")
    xl, z = f // 8, f % 8
    y, xh, c = d // 4, (d // 2) % 2, d % 2
    quad = z // 2
    mine = xl * 2 + z % 2

    def feat_at(r):
        return ((xl + r // 8) % 2) * 8 + (z + r % 8) % 8

    def feat_from(r):
        return ((xl + r // 8) % 2) * 8 + (z + 8 - r % 8) % 8

    def dp_at(r):
        return (d + r) % 16

    def send(src, dst, ss, rs, **where):
        return pltpu.make_async_remote_copy(
            src_ref=src, dst_ref=dst, send_sem=ss, recv_sem=rs, device_id=where, device_id_type=MESH
        )

    def loop(lo, hi, fn):
        def body(i, carry):
            fn(i)
            return carry

        lax.fori_loop(lo, hi, body, 0)

    feat_load = pltpu.make_async_copy(feats_hbm, feats, load_sem.at[0])
    feat_load.start()
    w2_load = pltpu.make_async_copy(w2_hbm, w2, load_sem.at[1])
    w2_load.start()
    w1_load = pltpu.make_async_copy(w1_hbm.at[y, c], w1.at[f, y, c], load_sem.at[2])
    w1_load.start()

    barrier = pltpu.get_barrier_semaphore()

    def greet(r):
        pl.semaphore_signal(barrier, inc=1, device_id={"feat": feat_at(r)}, device_id_type=MESH)
        pl.semaphore_signal(barrier, inc=1, device_id={"dp": dp_at(r)}, device_id_type=MESH)

    loop(1, 16, greet)

    headp[...] = jnp.zeros_like(headp)
    headp[:, 0:CLASSES] = head_ref[...]

    feat_load.wait()

    def widen(i):
        part = feats[pl.ds(i * 256, 256), :].astype(F32)
        tab[pl.ds(i * 256, 256), :] = jnp.concatenate([part, part], axis=1)

    loop(0, NODES // 256, widen)
    tab[pl.ds(NODES, 8), :] = jnp.zeros((8, 128), F32)

    w1_load.wait()
    pl.semaphore_wait(barrier, 30)

    def wa(r):
        return send(w1.at[f, y, c], w1.at[f, y, c], wa_s.at[r], wa_r.at[r], feat=feat_at(r))

    loop(1, 16, lambda r: wa(r).start())

    def wb(h, r):
        half = (xl + h) % 2
        spot = w1.at[pl.ds(half * 8, 8), y, c]
        return send(spot, spot, wb_s.at[h, r], wb_r.at[h, r], dp=((y + r) % 4) * 4 + xh * 2 + c)

    def wc(h):
        half = (xl + h) % 2
        spot = w1.at[pl.ds(half * 8, 8), :, c]
        return send(spot, spot, wc_s.at[h], wc_r.at[h], dp=y * 4 + xh * 2 + 1 - c)

    lane = lax.broadcasted_iota(jnp.int32, (1, 128), 1)
    left = lane < 64

    def gather(k):
        def body(g):
            for u in range(8):
                local = g * 8 + u
                t = k * ROWS + local
                vals = [tab[pl.ds(idx_ref[j, t], 1), :] for j in range(FAN1 + 1)]
                total = vals[1:]
                while len(total) > 1:
                    total = [
                        total[i] + total[i + 1] if i + 1 < len(total) else total[i]
                        for i in range(0, len(total), 2)
                    ]
                rows[pl.ds(local, 1), :] = jnp.where(left, vals[0], total[0] * inv_ref[0, t])

        loop(0, ROWS // 8, body)
        a4[mine, k] = rows[...].astype(BF16)

    lanes_f = pl.ds(pl.multiple_of(f * 128, 128), 128)

    def m1(r):
        return send(a4.at[mine, feat_at(r)], a_full.at[:, lanes_f], m1_s.at[r], m1_r.at[r], feat=feat_at(r))

    def block(r):
        gather(feat_at(r))
        m1(r).start()

        @pl.when(r == 5)
        def _():
            loop(1, 8, lambda i: wa(i).wait_recv())
            loop(1, 4, lambda i: wb(0, i).start())

        @pl.when(r == 8)
        def _():
            loop(8, 16, lambda i: wa(i).wait_recv())
            loop(1, 4, lambda i: wb(1, i).start())

        @pl.when(r == 12)
        def _():
            loop(1, 4, lambda i: wb(0, i).wait_recv())
            wc(0).start()

        @pl.when(r == 15)
        def _():
            loop(1, 4, lambda i: wb(1, i).wait_recv())
            wc(1).start()

    loop(1, 16, block)
    gather(f)
    a_full[:, lanes_f] = a4[mine, f]

    def mq(r):
        xq = (xl + r // 2) % 2
        zq = quad * 2 + (z + r) % 2
        return send(a4.at[mine], a4.at[mine], mq_s.at[r], mq_r.at[r], feat=xq * 8 + zq)

    loop(1, 4, lambda r: mq(r).start())

    loop(1, 16, lambda r: m1(r).wait_recv())
    loop(0, 2, lambda h: wc(h).wait_recv())

    def layer_one(n):
        cols = pl.ds(pl.multiple_of(n * 256, 256), 256)
        weight = w1[:, :, :, :, cols].reshape(2048, 256)
        out = jnp.dot(a_full[...], weight, preferred_element_type=F32)
        pre[:, cols] = out
        hidden_ref[:, cols] = (out * sigmoid(out)).astype(BF16)

    loop(0, 4, layer_one)

    counts = cnt_ref[...]
    count_float = counts.astype(F32)
    col = lax.broadcasted_iota(jnp.int32, (SEEDS, ROWS), 1)
    table = jnp.zeros((SEEDS, ROWS), F32)
    for j in range(FAN2):
        table = table + jnp.where((nbr_ref[:, j:j + 1] == col) & (j < counts), 1.0, 0.0)
    hidden = hidden_ref[...]
    seed_hidden = hidden[:SEEDS]
    neigh = (jnp.dot(table.astype(BF16), hidden, preferred_element_type=F32) / count_float).astype(BF16)

    w2_load.wait()
    both = jnp.concatenate([seed_hidden, neigh], axis=1)
    upper_pre = jnp.dot(both, w2[...], preferred_element_type=F32)
    upper_sigma = sigmoid(upper_pre)
    upper_hidden = (upper_pre * upper_sigma).astype(BF16)
    logits = jnp.dot(upper_hidden, headp[...], preferred_element_type=F32)
    logits_ref[...] = logits[:, 0:CLASSES]
    cls = lax.broadcasted_iota(jnp.int32, (SEEDS, 128), 1)
    live = cls < CLASSES
    top = jnp.max(jnp.where(live, logits, -jnp.inf), axis=1, keepdims=True)
    expo = jnp.where(live, jnp.exp(jnp.where(live, logits - top, 0.0)), 0.0)
    probability = expo / jnp.sum(expo, axis=1, keepdims=True)
    one_hot = jnp.where(cls == lab_ref[...], 1.0, 0.0)
    grad_logits = ((probability - one_hot) / 256.0).astype(BF16)

    wide_left = lax.broadcasted_iota(jnp.int32, (SEEDS, 128), 1) < 64
    for hx in range(2):
        for q in range(4):
            lo = hx * 512 + q * 128
            s = seed_hidden[:, lo:lo + 128].astype(F32)
            n = neigh[:, lo:lo + 128].astype(F32)
            even = jnp.where(wide_left, s, pltpu.roll(n, 64, 1)).astype(BF16)
            odd = jnp.where(wide_left, pltpu.roll(s, 64, 1), n).astype(BF16)
            for other in range(2):
                p_send[other, q, :, hx * 256:hx * 256 + 128] = even
                p_send[other, q, :, hx * 256 + 128:hx * 256 + 256] = odd
            p_send[hx, q, :, 512:640] = upper_hidden[:, lo:lo + 128]
            p_send[hx, q, :, 640:768] = grad_logits

    def m2(r):
        to = feat_at(r)
        return send(p_send.at[to // 8, (to % 8) // 2], p_recv.at[f], m2_s.at[r], m2_r.at[r], feat=to)

    loop(1, 16, lambda r: m2(r).start())
    p_recv[f] = p_send[xl, quad]

    back_hidden = lax.dot_general(grad_logits, headp[...], NT, preferred_element_type=F32)
    slope_two = upper_sigma + upper_pre * upper_sigma * (1.0 - upper_sigma)
    grad_upper = (back_hidden * slope_two).astype(BF16)
    back_two = lax.dot_general(grad_upper, w2[...], NT, preferred_element_type=F32)
    back = jnp.concatenate([back_two[:, 0:WIDE], back_two[:, WIDE:2 * WIDE] / count_float], axis=0)
    high = back.astype(BF16)
    low = (back - high.astype(F32)).astype(BF16)
    eye = jnp.where(lax.broadcasted_iota(jnp.int32, (SEEDS, ROWS), 0) == col, 1.0, 0.0)
    spread = jnp.concatenate([eye, table, eye, table], axis=0)
    back_rows = lax.dot_general(
        spread.astype(BF16), jnp.concatenate([high, low], axis=0), TN, preferred_element_type=F32
    )
    for j in range(4):
        for h in range(2):
            lo = (2 * j if h == 0 else 2 * ((j + 2) % 4) + 1) * 128
            cols = slice(lo, lo + 128)
            grad_pre = (back_rows[:, cols] * silu_slope(pre[:, cols])).astype(BF16)
            g_send[j, 0:ROWS, h * 128:h * 128 + 128] = grad_pre
            g_send[j, ROWS:ROWS + SEEDS, h * 128:h * 128 + 128] = grad_upper[:, cols]

    def m3(r):
        to = feat_at(r)
        return send(g_send.at[(to // 8) * 2 + to % 2], g_recv.at[f], m3_s.at[r], m3_r.at[r], feat=to)

    loop(1, 16, lambda r: m3(r).start())
    g_recv[f] = g_send[mine]

    loop(1, 16, lambda r: m2(r).wait_recv())
    every = p_recv[...].reshape(16 * SEEDS, 768)
    head_part = lax.dot_general(every[:, 640:768], every[:, 512:640], TN, preferred_element_type=F32)
    hd_send[...] = head_part[0:32].astype(BF16)

    def m5(r):
        return send(hd_send, hd_recv.at[d], m5_s.at[r], m5_r.at[r], dp=dp_at(r))

    loop(1, 16, lambda r: m5(r).start())
    hd_recv[d] = hd_send[...]

    loop(1, 4, lambda r: mq(r).wait_recv())
    loop(1, 16, lambda r: m3(r).wait_recv())
    g_all = g_recv[...]
    a_all = jnp.concatenate([a4[m].reshape(16 * ROWS, 128) for m in range(4)], axis=1)
    part_one = lax.dot_general(g_all[:, 0:ROWS].reshape(16 * ROWS, 256), a_all, TN, preferred_element_type=F32)
    part_two = lax.dot_general(
        g_all[:, ROWS:ROWS + SEEDS].reshape(16 * SEEDS, 256), every[:, 0:512], TN, preferred_element_type=F32
    )
    for i in range(4):
        for m in range(4):
            z_send[i, m, 0] = part_one[i * 64:i * 64 + 64, m * 128:m * 128 + 128].astype(BF16)
            z_send[i, m, 1] = part_two[i * 64:i * 64 + 64, m * 128:m * 128 + 128].astype(BF16)

    def final(n):
        i, m = n // 4, n % 4
        to_f = (m // 2) * 8 + quad * 2 + m % 2
        to_d = ((mine + 2 * (i // 2)) % 4) * 4 + (i // 2) * 2 + i % 2
        own = (to_f == f) & (to_d == d)
        return own, send(z_send.at[i, m], z_recv.at[d], m4_s.at[n], m4_r.at[d], feat=to_f, dp=to_d)

    def final_start(n):
        own, copy = final(n)

        @pl.when(jnp.logical_not(own))
        def _():
            copy.start()

        @pl.when(own)
        def _():
            z_recv[d] = z_send[n // 4, n % 4]

    loop(0, 16, final_start)

    def m5_in(r):
        m5(r).wait_recv()

    loop(1, 16, m5_in)
    head_sum = jnp.sum(hd_recv[...].astype(F32), axis=0)
    head_sum = jnp.where(f % 2 == 1, pltpu.roll(head_sum, 64, 1), head_sum)
    ghead_ref[...] = head_sum.T[0:64, 0:CLASSES]

    source = (y + 2 * xh) % 4

    def final_in(n):
        own = (source == mine) & (n == d)

        @pl.when(jnp.logical_not(own))
        def _():
            send(z_send.at[0, 0], z_recv.at[n], m4_s.at[0], m4_r.at[n], feat=f, dp=d).wait_recv()

    loop(0, 16, final_in)
    grads = jnp.sum(z_recv[...].astype(F32), axis=0)
    one_ref[...] = grads[0].T.reshape(2, 64, 64)
    two_ref[...] = grads[1].T.reshape(2, 64, 64)

    def left_all(r):
        wa(r).wait_send()
        m1(r).wait_send()
        m2(r).wait_send()
        m3(r).wait_send()
        m5(r).wait_send()

    loop(1, 16, left_all)
    for h in range(2):
        loop(1, 4, lambda r: wb(h, r).wait_send())
        wc(h).wait_send()
    loop(1, 4, lambda r: mq(r).wait_send())

    def final_left(n):
        own, copy = final(n)

        @pl.when(jnp.logical_not(own))
        def _():
            copy.wait_send()

    loop(0, 16, final_left)


def shards(
    node_feats, target_ids, layer_one_nbrs, layer_one_counts, layer_two_nbrs, layer_two_counts, labels,
    layer_one_weight, layer_two_weight, head_weight,
):
    one_counts = layer_one_counts[0]
    slots = jnp.arange(FAN1, dtype=jnp.int32)[:, None] < one_counts[None, :]
    picked = jnp.where(slots, layer_one_nbrs[0].T, NODES)
    idx = jnp.concatenate([target_ids, picked], axis=0)
    inv = 1.0 / one_counts.astype(F32)[None, :]
    vmem = pl.BlockSpec(memory_space=pltpu.VMEM)
    smem = pl.BlockSpec(memory_space=pltpu.SMEM)
    hbm = pl.BlockSpec(memory_space=pl.ANY)
    dma = pltpu.SemaphoreType.DMA
    hidden, logits, grad_one, grad_two, grad_head = pl.pallas_call(
        kernel,
        out_shape=(
            jax.ShapeDtypeStruct((ROWS, WIDE), BF16),
            jax.ShapeDtypeStruct((SEEDS, CLASSES), F32),
            jax.ShapeDtypeStruct((2, 64, 64), F32),
            jax.ShapeDtypeStruct((2, 64, 64), F32),
            jax.ShapeDtypeStruct((64, CLASSES), F32),
        ),
        in_specs=[smem, smem, hbm, hbm, hbm, vmem, vmem, vmem, vmem],
        out_specs=(vmem,) * 5,
        scratch_shapes=[
            pltpu.VMEM((NODES, 64), BF16),
            pltpu.VMEM((NODES + 8, 128), F32),
            pltpu.VMEM((ROWS, 128), F32),
            pltpu.VMEM((4, 16, ROWS, 128), BF16),
            pltpu.VMEM((ROWS, 2048), BF16),
            pltpu.VMEM((16, 4, 2, 16, WIDE), BF16),
            pltpu.VMEM((2 * WIDE, WIDE), BF16),
            pltpu.VMEM((WIDE, 128), BF16),
            pltpu.VMEM((ROWS, WIDE), F32),
            pltpu.VMEM((2, 4, SEEDS, 768), BF16),
            pltpu.VMEM((16, SEEDS, 768), BF16),
            pltpu.VMEM((4, ROWS + SEEDS, 256), BF16),
            pltpu.VMEM((16, ROWS + SEEDS, 256), BF16),
            pltpu.VMEM((4, 4, 2, 64, 128), BF16),
            pltpu.VMEM((16, 2, 64, 128), BF16),
            pltpu.VMEM((32, 128), BF16),
            pltpu.VMEM((16, 32, 128), BF16),
            dma((3,)),
            dma((16,)), dma((16,)),
            dma((2, 4)), dma((2, 4)),
            dma((2,)), dma((2,)),
            dma((16,)), dma((16,)),
            dma((4,)), dma((4,)),
            dma((16,)), dma((16,)),
            dma((16,)), dma((16,)),
            dma((16,)), dma((16,)),
            dma((16,)), dma((16,)),
        ],
        compiler_params=pltpu.CompilerParams(
            collective_id=0, has_side_effects=True, vmem_limit_bytes=48 * 1024 * 1024
        ),
        name="step",
    )(
        idx, inv, node_feats[0], layer_one_weight.reshape(4, 2, 16, WIDE), layer_two_weight.reshape(2 * WIDE, WIDE),
        head_weight, layer_two_nbrs[0], layer_two_counts.reshape(SEEDS, 1), labels.reshape(SEEDS, 1),
    )
    return hidden[None], logits[None], grad_one, grad_two, grad_head


def solution(mesh):
    return jax.shard_map(
        shards,
        mesh=mesh,
        in_specs=(
            P("dp", None, "feat"),
            P("dp", None),
            P("dp", None, None),
            P("dp", None),
            P("dp", "feat", None),
            P("dp", "feat"),
            P("dp", "feat"),
            P(None, "feat", None),
            P(),
            P(),
        ),
        out_specs=(
            P("dp", "feat", None),
            P("dp", "feat", None),
            P(None, "feat", "dp"),
            P(None, "feat", "dp"),
            P("feat", None),
        ),
        check_vma=False,
    )
```

```python
import functools

import jax
import jax.numpy as jnp
from jax import lax
from jax.experimental import pallas as pl
from jax.experimental.pallas import tpu as pltpu
from jax.sharding import PartitionSpec as P

MESH = pl.DeviceIdType.MESH
BF16 = jnp.bfloat16
F32 = jnp.float32

NODES = 6144
ROWS = 96
SEEDS = 16
FAN1 = 10
FAN2 = 5
CLASSES = 19
WIDE = 1024
WB0, WB1, WC0, WC1 = 3, 8, 12, 15
TN = (((0,), (0,)), ((), ()))
NT = (((1,), (1,)), ((), ()))


def sigmoid(values):
    return 1.0 / (1.0 + jnp.exp(-values))


def silu_slope(values):
    sigma = sigmoid(values)
    return sigma + values * sigma * (1.0 - sigma)


def kernel(
    self_ref, one_nbr_ref, one_cnt_ref, feats_hbm, w1_hbm, w2_hbm, head_ref, nbr_ref, cnt_ref, lab_ref,
    hidden_ref, logits_ref, one_ref, two_ref, ghead_ref,
    idx_vmem, idx_ref, inv_vmem, inv_ref, feats, tab, rows, a_send, a_pool, w1, w2, headp, pre,
    p_send, p_recv, sn_send, sn_pool, g_send, g_pool, gu_all, x1_send, x1_recv, z1_send, z1_recv, x2_send, x2_recv,
    hd_send, hd_recv,
    load_sem, wa_s, wa_r, wb_s, wb_r, wx_s, wx_r, wc_s, wc_r, m1_s, m1_r, ma_s, ma_r, ms_s, ms_r, m2_s, m2_r,
    sz_s, sz_r, sy_s, sy_r, sc_s, sc_r, m3_s, m3_r, gz_s, gz_r, x1_s, x1_r, z1_s, z1_r, x2_s, x2_r, m5_s, m5_r,
):
    f = lax.axis_index("feat")
    d = lax.axis_index("dp")
    xl, z = f // 8, f % 8
    y, xh, c = d // 4, (d // 2) % 2, d % 2
    x = xh * 2 + xl
    quad = z // 2

    def feat_at(r):
        return ((xl + r // 8) % 2) * 8 + (z + r % 8) % 8

    def feat_from(r):
        return ((xl + r // 8) % 2) * 8 + (z + 8 - r % 8) % 8

    def z_at(r):
        return xl * 8 + (z + r) % 8

    def y_at(r):
        return ((y + r) % 4) * 4 + xh * 2 + c

    def x_at(r):
        to = (x + r) % 4
        return {"feat": (to % 2) * 8 + z, "dp": y * 4 + (to // 2) * 2 + c}

    def yc_at(r):
        return (y + r // 2) % 4, (c + r % 2) % 2

    sibling = y * 4 + xh * 2 + 1 - c

    def send(src, dst, ss, rs, **where):
        return pltpu.make_async_remote_copy(
            src_ref=src, dst_ref=dst, send_sem=ss, recv_sem=rs, device_id=where, device_id_type=MESH
        )

    def loop(lo, hi, fn):
        def body(i, carry):
            fn(i)
            return carry

        lax.fori_loop(lo, hi, body, 0)

    waits = {}

    def now(name):
        waits.pop(name)()

    def comm(name, lo, hi, make, start=True):
        if start:
            loop(lo, hi, lambda r: make(r).start())
        waits[name + "_s"] = lambda: loop(lo, hi, lambda r: make(r).wait_send())
        waits[name + "_r"] = lambda: loop(lo, hi, lambda r: make(r).wait_recv())

    barrier = pltpu.get_barrier_semaphore()

    def greet(r):
        pl.semaphore_signal(barrier, inc=1, device_id={"feat": feat_at(r)}, device_id_type=MESH)
        pl.semaphore_signal(barrier, inc=1, device_id={"dp": (d + r) % 16}, device_id_type=MESH)

    loop(1, 16, greet)
    corner = {"feat": (1 - xl) * 8 + z, "dp": y * 4 + (1 - xh) * 2 + c}
    pl.semaphore_signal(barrier, inc=1, device_id=corner, device_id_type=MESH)

    w1_load = pltpu.make_async_copy(w1_hbm.at[y, c], w1.at[xl, z, y, c], load_sem.at[2])
    w1_load.start()

    def feat_load(i):
        part = pl.ds(pl.multiple_of(i * 1024, 1024), 1024)
        return pltpu.make_async_copy(feats_hbm.at[:, part], feats.at[:, part], load_sem.at[4 + i])

    loop(0, 6, lambda i: feat_load(i).start())
    w2_load = pltpu.make_async_copy(w2_hbm, w2, load_sem.at[1])
    w2_load.start()
    waits["w2"] = lambda: w2_load.wait()

    one_counts = one_cnt_ref[...]
    for j in range(FAN1):
        idx_vmem[j] = jnp.where(j < one_counts, one_nbr_ref[j], NODES)
    inv_vmem[...] = 1.0 / one_counts.astype(F32)
    idx_load = pltpu.make_async_copy(idx_vmem, idx_ref, load_sem.at[0])
    idx_load.start()
    inv_load = pltpu.make_async_copy(inv_vmem, inv_ref, load_sem.at[3])
    inv_load.start()
    headp[...] = jnp.zeros_like(headp)
    headp[0:CLASSES, :] = head_ref[...]

    def wa(r):
        return send(w1.at[xl, z, y, c], w1.at[xl, z, y, c], wa_s.at[r], wa_r.at[r], feat=z_at(r))

    w1_load.wait()
    pl.semaphore_wait(barrier, 31)
    comm("wa", 1, 8, wa)

    def widen(i):
        feat_load(i).wait()

        def tile(t):
            first = pl.multiple_of(i * 1024 + t * 128, 128)
            part = feats[:, pl.ds(first, 128)].astype(F32)
            tab[pl.ds(first, 128), :] = jnp.concatenate([part, part], axis=0).T

        loop(0, 8, tile)

    loop(0, 6, widen)
    tab[pl.ds(NODES, 8), :] = jnp.zeros((8, 128), F32)
    idx_load.wait()
    inv_load.wait()

    def wb(g, r):
        spot = w1.at[xl, pl.ds(((xh + g) % 2) * 4, 4), y, c]
        return send(spot, spot, wb_s.at[g, r], wb_r.at[g, r], dp=y_at(r))

    def wx(n):
        r, s = n // 2, n % 2
        spot = w1.at[xl, pl.ds(xh * 4, 4), (y + 4 - r) % 4, c]
        return send(spot, spot, wx_s.at[n], wx_r.at[n], **x_at(1 + 2 * s))

    def wc(g):
        spot = w1.at[(xl + g) % 2, :, :, c]
        return send(spot, spot, wc_s.at[g], wc_r.at[g], dp=sibling)

    lane = lax.broadcasted_iota(jnp.int32, (1, 128), 1)
    left = lane < 64

    def gather(k):
        def body(g):
            for u in range(8):
                local = g * 8 + u
                t = k * ROWS + local
                own = tab[pl.ds(self_ref[0, t], 1), :]
                total = [tab[pl.ds(idx_ref[j, 0, t], 1), :] for j in range(FAN1)]
                while len(total) > 1:
                    total = [
                        total[i] + total[i + 1] if i + 1 < len(total) else total[i]
                        for i in range(0, len(total), 2)
                    ]
                rows[pl.ds(local, 1), :] = jnp.where(left, own, total[0] * inv_ref[0, t])

        loop(0, ROWS // 8, body)
        a_send[k] = rows[...].astype(BF16)

    def lanes(block):
        return pl.ds(pl.multiple_of(block * 128, 128), 128)

    def m1(r):
        return send(a_send.at[feat_at(r)], a_pool.at[y, c, :, lanes(f)], m1_s.at[r], m1_r.at[r], feat=feat_at(r))

    def ma(r, i):
        spot = a_pool.at[y, c, :, lanes(feat_from(r))]
        return send(spot, spot, ma_s.at[r, i], ma_r.at[i], dp=y_at(i))

    def pass_on(r):
        m1(r).wait_recv()
        loop(1, 4, lambda i: ma(r, i).start())

    def block(r):
        gather(feat_at(r))
        m1(r).start()

        @pl.when(r == WB0)
        def _():
            now("wa_r")
            loop(1, 4, lambda i: wb(0, i).start())
            loop(0, 2, lambda n: wx(n).start())

        @pl.when(r == WB1)
        def _():
            loop(1, 4, lambda i: wb(0, i).wait_recv())
            loop(2, 8, lambda n: wx(n).start())
            loop(1, 4, lambda i: wb(1, i).start())

        @pl.when(r >= 9)
        def _():
            pass_on(2 * r - 17)
            pass_on(2 * r - 16)

        @pl.when(r == WC0)
        def _():
            loop(1, 4, lambda i: wb(1, i).wait_recv())
            wc(0).start()

        @pl.when(r == WC1)
        def _():
            loop(0, 8, lambda n: wx(n).wait_recv())
            wc(1).start()

    loop(1, 16, block)
    waits["wb_s"] = lambda: [loop(1, 4, lambda r, g=g: wb(g, r).wait_send()) for g in range(2)]
    comm("wc", 0, 2, wc, False)
    waits["wx_s"] = lambda: loop(0, 8, lambda n: wx(n).wait_send())
    waits["m1_s"] = lambda: loop(1, 16, lambda r: m1(r).wait_send())
    gather(f)
    a_pool[y, c, :, lanes(f)] = a_send[f]
    loop(1, 4, lambda i: ma(0, i).start())
    pass_on(15)
    waits["ma_s"] = lambda: loop(0, 16, lambda r: loop(1, 4, lambda i: ma(r, i).wait_send()))

    def ma_wait(i):
        send(a_pool.at[y, c], a_pool.at[y, c], ma_s.at[0, i], ma_r.at[i], dp=y_at(i)).wait_recv()

    waits["ma_r"] = lambda: loop(1, 4, ma_wait)
    now("wc_r")

    def layer_one(n):
        cols = pl.ds(pl.multiple_of(n * 256, 256), 256)
        weight = w1[:, :, :, :, :, cols].reshape(2048, 256)
        out = jnp.dot(a_pool[y, c], weight, preferred_element_type=F32)
        pre[:, cols] = out
        hidden_ref[:, cols] = (out * sigmoid(out)).astype(BF16)

    loop(0, 4, layer_one)

    eye = lax.broadcasted_iota(jnp.int32, (SEEDS, SEEDS), 0) == lax.broadcasted_iota(jnp.int32, (SEEDS, SEEDS), 1)

    def column(row):
        return jnp.sum(jnp.where(eye, row, 0), axis=1, keepdims=True)

    counts = column(cnt_ref[...])
    count_float = counts.astype(F32)
    col = lax.broadcasted_iota(jnp.int32, (SEEDS, ROWS), 1)
    table = jnp.zeros((SEEDS, ROWS), F32)
    for j in range(FAN2):
        table = table + jnp.where((column(nbr_ref[j]) == col) & (j < counts), 1.0, 0.0)
    hidden = hidden_ref[...]
    seed_hidden = hidden[:SEEDS]
    neigh = (jnp.dot(table.astype(BF16), hidden, preferred_element_type=F32) / count_float).astype(BF16)

    wide_left = lax.broadcasted_iota(jnp.int32, (SEEDS, 128), 1) < 64
    for hx in range(2):
        for q in range(4):
            lo = hx * 512 + q * 128
            s = seed_hidden[:, lo:lo + 128].astype(F32)
            n = neigh[:, lo:lo + 128].astype(F32)
            here = slice(hx * 128, hx * 128 + 128)
            sn_send[2 * q, :, here] = jnp.where(wide_left, s, pltpu.roll(n, 64, 1)).astype(BF16)
            sn_send[2 * q + 1, :, here] = jnp.where(wide_left, pltpu.roll(s, 64, 1), n).astype(BF16)

    def sz(r):
        return send(sn_send.at[(z + r) % 8], sn_pool.at[z, y, c], sz_s.at[r], sz_r.at[r], feat=z_at(r))

    comm("sz", 1, 8, sz)
    sn_pool[z, y, c] = sn_send[z]

    now("w2")
    both = jnp.concatenate([seed_hidden, neigh], axis=1)
    upper_pre = jnp.dot(both, w2[...], preferred_element_type=F32)
    upper_sigma = sigmoid(upper_pre)
    upper_hidden = (upper_pre * upper_sigma).astype(BF16)
    logits = lax.dot_general(upper_hidden, headp[...], NT, preferred_element_type=F32)
    logits_ref[...] = logits[:, 0:CLASSES]
    cls = lax.broadcasted_iota(jnp.int32, (SEEDS, 128), 1)
    live = cls < CLASSES
    top = jnp.max(jnp.where(live, logits, -jnp.inf), axis=1, keepdims=True)
    expo = jnp.where(live, jnp.exp(jnp.where(live, logits - top, 0.0)), 0.0)
    probability = expo / jnp.sum(expo, axis=1, keepdims=True)
    one_hot = jnp.where(cls == column(lab_ref[...]), 1.0, 0.0)
    grad_logits = ((probability - one_hot) / 256.0).astype(BF16)

    for hx in range(2):
        for q in range(4):
            lo = hx * 512 + q * 128
            p_send[hx, q, :, 0:128] = upper_hidden[:, lo:lo + 128]
            p_send[hx, q, :, 128:256] = grad_logits

    def m2(r):
        to = feat_at(r)
        return send(p_send.at[to // 8, (to % 8) // 2], p_recv.at[f], m2_s.at[r], m2_r.at[r], feat=to)

    comm("m2", 1, 16, m2)
    p_recv[f] = p_send[xl, quad]

    back_hidden = jnp.dot(grad_logits, headp[...], preferred_element_type=F32)
    slope_two = upper_sigma + upper_pre * upper_sigma * (1.0 - upper_sigma)
    grad_upper = (back_hidden * slope_two).astype(BF16)
    back_two = lax.dot_general(grad_upper, w2[...], NT, preferred_element_type=F32)
    back = jnp.concatenate([back_two[:, 0:WIDE], back_two[:, WIDE:2 * WIDE] / count_float], axis=0)
    high = back.astype(BF16)
    low = (back - high.astype(F32)).astype(BF16)
    first = jnp.where(lax.broadcasted_iota(jnp.int32, (SEEDS, ROWS), 0) == col, 1.0, 0.0)
    spread = jnp.concatenate([first, table, first, table], axis=0)
    back_rows = lax.dot_general(
        spread.astype(BF16), jnp.concatenate([high, low], axis=0), TN, preferred_element_type=F32
    )
    tall_left = lax.broadcasted_iota(jnp.int32, (ROWS + SEEDS, 128), 1) < 64
    for to_y in range(4):
        half = []
        for to_x in range(2):
            cols = slice(to_y * 256 + to_x * 128, to_y * 256 + to_x * 128 + 128)
            grad_pre = back_rows[:, cols] * silu_slope(pre[:, cols])
            half.append(jnp.concatenate([grad_pre, grad_upper[:, cols].astype(F32)], axis=0))
        g_send[to_y, 0] = jnp.where(tall_left, half[0], pltpu.roll(half[1], 64, 1)).astype(BF16)
        g_send[to_y, 1] = jnp.where(tall_left, pltpu.roll(half[0], 64, 1), half[1]).astype(BF16)

    def m3(r):
        to_y, to_c = yc_at(r)
        return send(
            g_send.at[to_y, to_c], g_pool.at[y, c], m3_s.at[r], m3_r.at[r], dp=to_y * 4 + xh * 2 + to_c
        )

    comm("m3", 1, 8, m3)
    g_pool[y, c] = g_send[y, c]

    def ms(n):
        spot = a_pool.at[:, c]
        return send(spot, spot, ms_s.at[n], ms_r.at[n], dp=sibling)

    now("ma_r")
    comm("ms", 0, 1, ms)

    def sy(r):
        spot = sn_pool.at[:, y, c]
        return send(spot, spot, sy_s.at[r], sy_r.at[r], dp=y_at(r))

    def sc(n):
        spot = sn_pool.at[:, :, c]
        return send(spot, spot, sc_s.at[n], sc_r.at[n], dp=sibling)

    now("sz_r")
    comm("sy", 1, 4, sy)

    now("m3_r")
    gu_all[z] = g_pool[:, :, ROWS:ROWS + SEEDS]

    def gz(r):
        return send(gu_all.at[z], gu_all.at[z], gz_s.at[r], gz_r.at[r], feat=z_at(r))

    comm("gz", 1, 8, gz)

    now("ms_r")
    part_one = lax.dot_general(
        g_pool[:, :, 0:ROWS].reshape(8 * ROWS, 128), a_pool[...].reshape(8 * ROWS, 2048), TN,
        preferred_element_type=F32,
    ).astype(BF16)
    for to_h in range(2):
        for to_l in range(2):
            x1_send[to_h, to_l] = part_one[to_h * 64:to_h * 64 + 64, to_l * 1024:to_l * 1024 + 1024]

    def x1(r):
        to = (x + r) % 4
        return send(x1_send.at[to // 2, to % 2], x1_recv.at[x], x1_s.at[r], x1_r.at[r], **x_at(r))

    comm("x1", 1, 4, x1)
    x1_recv[x] = x1_send[xh, xl]

    now("sy_r")
    comm("sc", 0, 1, sc)
    now("m2_r")
    every = p_recv[...].reshape(16 * SEEDS, 256)
    head_part = lax.dot_general(every[:, 128:256], every[:, 0:128], TN, preferred_element_type=F32)
    hd_send[...] = head_part[0:32].astype(BF16)

    def m5(r):
        return send(hd_send, hd_recv.at[d], m5_s.at[r], m5_r.at[r], dp=(d + r) % 16)

    comm("m5", 1, 16, m5)
    hd_recv[d] = hd_send[...]

    now("sc_r")
    now("gz_r")
    part_two = lax.dot_general(
        gu_all[...].reshape(64 * SEEDS, 128), sn_pool[...].reshape(64 * SEEDS, 256), TN, preferred_element_type=F32
    ).astype(BF16)
    for to_h in range(2):
        for to_l in range(2):
            x2_send[to_h, to_l] = part_two[to_h * 64:to_h * 64 + 64, to_l * 128:to_l * 128 + 128]

    def x2(r):
        to = (x + r) % 4
        return send(x2_send.at[to // 2, to % 2], x2_recv.at[x], x2_s.at[r], x2_r.at[r], **x_at(r))

    comm("x2", 1, 4, x2)
    x2_recv[x] = x2_send[xh, xl]

    now("x1_r")
    sum_x = jnp.sum(x1_recv[...].astype(F32), axis=0).astype(BF16)
    for to_z in range(8):
        z1_send[to_z] = sum_x[:, to_z * 128:to_z * 128 + 128]

    def z1(r):
        return send(z1_send.at[(z + r) % 8], z1_recv.at[z], z1_s.at[r], z1_r.at[r], feat=z_at(r))

    comm("z1", 1, 8, z1)
    z1_recv[z] = z1_send[z]

    now("m5_r")
    head_sum = jnp.sum(hd_recv[...].astype(F32), axis=0)
    head_sum = jnp.where(f % 2 == 1, pltpu.roll(head_sum, 64, 1), head_sum)
    ghead_ref[...] = head_sum[0:CLASSES, 0:64]

    now("x2_r")
    two_ref[...] = jnp.sum(x2_recv[...].astype(F32), axis=0).T.reshape(2, 64, 64)
    now("z1_r")
    one_ref[...] = jnp.sum(z1_recv[...].astype(F32), axis=0).T.reshape(2, 64, 64)

    for wait in waits.values():
        wait()


def shards(
    node_feats, target_ids, layer_one_nbrs, layer_one_counts, layer_two_nbrs, layer_two_counts, labels,
    layer_one_weight, layer_two_weight, head_weight,
):
    vmem = pl.BlockSpec(memory_space=pltpu.VMEM)
    smem = pl.BlockSpec(memory_space=pltpu.SMEM)
    hbm = pl.BlockSpec(memory_space=pltpu.HBM)
    dma = pltpu.SemaphoreType.DMA
    hidden, logits, grad_one, grad_two, grad_head = pl.pallas_call(
        kernel,
        out_shape=(
            jax.ShapeDtypeStruct((ROWS, WIDE), BF16),
            jax.ShapeDtypeStruct((SEEDS, CLASSES), F32),
            jax.ShapeDtypeStruct((2, 64, 64), F32),
            jax.ShapeDtypeStruct((2, 64, 64), F32),
            jax.ShapeDtypeStruct((CLASSES, 64), F32),
        ),
        in_specs=[smem, vmem, vmem, hbm, hbm, hbm, vmem, vmem, vmem, vmem],
        out_specs=(vmem,) * 5,
        scratch_shapes=[
            pltpu.VMEM((FAN1, 1, 16 * ROWS), jnp.int32),
            pltpu.SMEM((FAN1, 1, 16 * ROWS), jnp.int32),
            pltpu.VMEM((1, 16 * ROWS), F32),
            pltpu.SMEM((1, 16 * ROWS), F32),
            pltpu.VMEM((64, NODES), BF16),
            pltpu.VMEM((NODES + 8, 128), F32),
            pltpu.VMEM((ROWS, 128), F32),
            pltpu.VMEM((16, ROWS, 128), BF16),
            pltpu.VMEM((4, 2, ROWS, 2048), BF16),
            pltpu.VMEM((2, 8, 4, 2, 16, WIDE), BF16),
            pltpu.VMEM((2 * WIDE, WIDE), BF16),
            pltpu.VMEM((128, WIDE), BF16),
            pltpu.VMEM((ROWS, WIDE), F32),
            pltpu.VMEM((2, 4, SEEDS, 256), BF16),
            pltpu.VMEM((16, SEEDS, 256), BF16),
            pltpu.VMEM((8, SEEDS, 256), BF16),
            pltpu.VMEM((8, 4, 2, SEEDS, 256), BF16),
            pltpu.VMEM((4, 2, ROWS + SEEDS, 128), BF16),
            pltpu.VMEM((4, 2, ROWS + SEEDS, 128), BF16),
            pltpu.VMEM((8, 4, 2, SEEDS, 128), BF16),
            pltpu.VMEM((2, 2, 64, 1024), BF16),
            pltpu.VMEM((4, 64, 1024), BF16),
            pltpu.VMEM((8, 64, 128), BF16),
            pltpu.VMEM((8, 64, 128), BF16),
            pltpu.VMEM((2, 2, 64, 128), BF16),
            pltpu.VMEM((4, 64, 128), BF16),
            pltpu.VMEM((32, 128), BF16),
            pltpu.VMEM((16, 32, 128), BF16),
            dma((10,)),
            dma((8,)), dma((8,)),
            dma((2, 4)), dma((2, 4)),
            dma((8,)), dma((8,)),
            dma((2,)), dma((2,)),
            dma((16,)), dma((16,)),
            dma((16, 4)), dma((4,)),
            dma((1,)), dma((1,)),
            dma((16,)), dma((16,)),
            dma((8,)), dma((8,)),
            dma((4,)), dma((4,)),
            dma((1,)), dma((1,)),
            dma((8,)), dma((8,)),
            dma((8,)), dma((8,)),
            dma((4,)), dma((4,)),
            dma((8,)), dma((8,)),
            dma((4,)), dma((4,)),
            dma((16,)), dma((16,)),
        ],
        compiler_params=pltpu.CompilerParams(
            collective_id=0, has_side_effects=True, vmem_limit_bytes=60 * 1024 * 1024
        ),
        name="step",
    )(
        target_ids, layer_one_nbrs.transpose(2, 0, 1), layer_one_counts, node_feats[0].T,
        layer_one_weight.reshape(4, 2, 16, WIDE), layer_two_weight.reshape(2 * WIDE, WIDE), head_weight.T,
        layer_two_nbrs.transpose(2, 0, 1), layer_two_counts, labels,
    )
    return hidden[None], logits[None], grad_one, grad_two, grad_head.T


def solution(mesh):
    return jax.shard_map(
        shards,
        mesh=mesh,
        in_specs=(
            P("dp", None, "feat"),
            P("dp", None),
            P("dp", None, None),
            P("dp", None),
            P("dp", "feat", None),
            P("dp", "feat"),
            P("dp", "feat"),
            P(None, "feat", None),
            P(),
            P(),
        ),
        out_specs=(
            P("dp", "feat", None),
            P("dp", "feat", None),
            P(None, "feat", "dp"),
            P(None, "feat", "dp"),
            P("feat", None),
        ),
        check_vma=False,
    )
```

```python
import functools

import jax
import jax.numpy as jnp
from jax import lax
from jax.experimental import pallas as pl
from jax.experimental.pallas import tpu as pltpu
from jax.sharding import PartitionSpec as P

MESH = pl.DeviceIdType.MESH
BF16 = jnp.bfloat16
F32 = jnp.float32

NODES = 6144
ROWS = 96
TARGETS = 16 * ROWS
UNROLL = 16
SEEDS = 16
FAN1 = 10
FAN2 = 5
CLASSES = 19
WIDE = 1024
LAG, LAG_F, LAG_C, TO_X = 6, 9, 12, 13
TN = (((0,), (0,)), ((), ()))
NT = (((1,), (1,)), ((), ()))


def sigmoid(values):
    return 1.0 / (1.0 + jnp.exp(-values))


def silu_slope(values):
    sigma = sigmoid(values)
    return sigma + values * sigma * (1.0 - sigma)


def kernel(
    self_ref, one_nbr_ref, one_cnt_ref, feats_hbm, w1_hbm, w2_hbm, head_ref, nbr_ref, cnt_ref, lab_ref,
    hidden_ref, logits_ref, one_ref, two_ref, ghead_ref,
    idx_vmem, idx_ref, inv_vmem, inv_ref, feats, tab, rows, a_send, a_pool, w1, w2, headp, pre, h_send, hidden_vmem,
    p_send, p_recv, sn_send, sn_pool, b_send, b_pool, g_pool, gu_all, g_turned,
    x1_send, x1_recv, z1_send, z1_recv, x2_send, x2_recv, hd_send, hd_recv,
    load_sem, wa_s, wa_r, wx_s, wx_r, m1_s, m1_r, ma_s, ma_r, ms_s, ms_r, h_s, h_r, m2_s, m2_r,
    sz_s, sz_r, sy_s, sy_r, sc_s, sc_r, m3_s, m3_r, gz_s, gz_r, x1_s, x1_r, z1_s, z1_r, x2_s, x2_r, m5_s, m5_r,
):
    f = lax.axis_index("feat")
    d = lax.axis_index("dp")
    xl, z = f // 8, f % 8
    y, xh, c = d // 4, (d // 2) % 2, d % 2
    x = xh * 2 + xl
    quad = z // 2

    def feat_at(r):
        return ((xl + r // 8) % 2) * 8 + (z + r % 8) % 8

    def feat_from(r):
        return ((xl + r // 8) % 2) * 8 + (z + 8 - r % 8) % 8

    def z_at(r):
        return xl * 8 + (z + r) % 8

    def y_at(r):
        return ((y + r) % 4) * 4 + xh * 2 + c

    def x_at(r):
        to = (x + r) % 4
        return {"feat": (to % 2) * 8 + z, "dp": y * 4 + (to // 2) * 2 + c}

    def yc_at(r):
        return (y + r // 2) % 4, (c + r % 2) % 2

    sibling = y * 4 + xh * 2 + 1 - c

    def send(src, dst, ss, rs, **where):
        return pltpu.make_async_remote_copy(
            src_ref=src, dst_ref=dst, send_sem=ss, recv_sem=rs, device_id=where, device_id_type=MESH
        )

    def loop(lo, hi, fn):
        def body(i, carry):
            fn(i)
            return carry

        lax.fori_loop(lo, hi, body, 0)

    def lanes(block):
        return pl.ds(pl.multiple_of(block * 128, 128), 128)

    waits = {}

    def now(name):
        waits.pop(name)()

    def comm(name, lo, hi, make, start=True):
        if start:
            loop(lo, hi, lambda r: make(r).start())
        waits[name + "_s"] = lambda: loop(lo, hi, lambda r: make(r).wait_send())
        waits[name + "_r"] = lambda: loop(lo, hi, lambda r: make(r).wait_recv())

    barrier = pltpu.get_barrier_semaphore()

    def greet(r):
        pl.semaphore_signal(barrier, inc=1, device_id={"feat": feat_at(r)}, device_id_type=MESH)
        pl.semaphore_signal(barrier, inc=1, device_id={"dp": (d + r) % 16}, device_id_type=MESH)

    loop(1, 16, greet)
    for n in range(1, 4):
        corner = {"feat": (1 - xl) * 8 + z, "dp": y * 4 + ((xh + n // 2) % 2) * 2 + (c + n % 2) % 2}
        pl.semaphore_signal(barrier, inc=1, device_id=corner, device_id_type=MESH)

    w1_load = pltpu.make_async_copy(w1_hbm.at[:, lanes(y * 2 + c)], w1.at[xl, z], load_sem.at[2])
    w1_load.start()
    waits["w1"] = lambda: w1_load.wait()

    def feat_load(i):
        part = pl.ds(pl.multiple_of(i * 1024, 1024), 1024)
        return pltpu.make_async_copy(feats_hbm.at[:, part], feats.at[:, part], load_sem.at[4 + i])

    loop(0, 6, lambda i: feat_load(i).start())
    waits["feats"] = lambda: loop(0, 6, lambda i: feat_load(i).wait())
    w2_load = pltpu.make_async_copy(w2_hbm, w2, load_sem.at[1])
    w2_load.start()
    waits["w2"] = lambda: w2_load.wait()

    one_counts = one_cnt_ref[...]
    for j in range(FAN1):
        idx_vmem[:, j * TARGETS:(j + 1) * TARGETS] = jnp.where(j < one_counts, one_nbr_ref[j], NODES)
    inv_vmem[...] = 1.0 / one_counts.astype(F32)
    idx_load = pltpu.make_async_copy(idx_vmem, idx_ref, load_sem.at[0])
    idx_load.start()
    waits["idx"] = lambda: idx_load.wait()
    inv_load = pltpu.make_async_copy(inv_vmem, inv_ref, load_sem.at[3])
    inv_load.start()
    waits["inv"] = lambda: inv_load.wait()
    headp[...] = jnp.zeros_like(headp)
    headp[0:CLASSES, :] = head_ref[...]

    def wa(r):
        return send(w1.at[xl, z], w1.at[xl, z], wa_s.at[r], wa_r.at[r], feat=z_at(r))

    def wx(n):
        spot = w1.at[xl, pl.ds(xh * 4, 4)]
        return send(spot, spot, wx_s.at[n], wx_r.at[n], **x_at(1 + 2 * n))

    now("w1")
    pl.semaphore_wait(barrier, 33)
    comm("wa", 1, 8, wa)

    waits.pop("feats")

    for i in range(6):
        feat_load(i).wait()
        for first in range(i * 1024, i * 1024 + 1024, 128):
            part = feats[:, first:first + 128]
            tab[first:first + 128, :] = jnp.concatenate([part, part], axis=0).T.astype(F32)
    tab[pl.ds(NODES, 8), :] = jnp.zeros((8, 128), F32)
    now("idx")
    now("inv")

    lane = lax.broadcasted_iota(jnp.int32, (1, 128), 1)
    left = lane < 64

    def gather(k):
        def body(g):
            for u in range(UNROLL):
                local = g * UNROLL + u
                t = k * ROWS + local
                own = tab[pl.ds(self_ref[0, t], 1), :]
                total = [tab[pl.ds(idx_ref[0, j * TARGETS + t], 1), :] for j in range(FAN1)]
                while len(total) > 1:
                    total = [
                        total[i] + total[i + 1] if i + 1 < len(total) else total[i]
                        for i in range(0, len(total), 2)
                    ]
                rows[pl.ds(local, 1), :] = jnp.where(left, own, total[0] * inv_ref[0, t])

        loop(0, ROWS // UNROLL, body)
        a_send[k] = rows[...].astype(BF16)

    def m1(r):
        return send(a_send.at[feat_at(r)], a_pool.at[y, c, :, lanes(f)], m1_s.at[r], m1_r.at[r], feat=feat_at(r))

    def ma(r, i):
        spot = a_pool.at[y, c, :, lanes(feat_from(r))]
        return send(spot, spot, ma_s.at[r, i], ma_r.at[r, i], dp=y_at(i))

    def pass_two(step, r):
        after = 1 + 2 * (step % 2)
        ma(r, after).wait_recv()
        spot = a_pool.at[(y + 4 - after) % 4, c, :, lanes(feat_from(r))]
        return send(spot, spot, ma_s.at[r, 2], ma_r.at[r, 2], dp=y_at(after))

    def ma_wait(step, r):
        ma(r, 3 - 2 * (step % 2)).wait_recv()
        ma(r, 2).wait_recv()

    def ms(r):
        spot = a_pool.at[:, c, :, lanes(feat_from(r))]
        return send(spot, spot, ms_s.at[r], ms_r.at[0], dp=sibling)

    def pass_on(step):
        r = peer(step)
        m1(r).wait_recv()
        loop(0, 2, lambda i: ma(r, 1 + 2 * i).start())

    def forward(step):
        pass_two(step, peer(step)).start()

    def cross(step):
        r = peer(step)
        ma_wait(step, r)
        ms(r).start()

    def peer(step):
        t = step + 1
        far = 4 - t // 4
        sign, rx = (t % 4) // 2, (t + t // 16) % 2
        return rx * 8 + (far * (1 - sign) + (8 - far) * sign) % 8

    def block(step):
        r = peer(step)
        gather(feat_at(r))
        m1(r).start()
        pl.when(step > LAG)(lambda: pass_on(step - LAG))
        pl.when(step == LAG_F)(forward_own)
        pl.when(step > LAG_F)(lambda: forward(step - LAG_F))
        pl.when(step == LAG_C)(cross_own)
        pl.when(step > LAG_C)(lambda: cross(step - LAG_C))

        @pl.when(step == TO_X)
        def _():
            now("wa_r")
            loop(0, 2, lambda n: wx(n).start())

    def forward_own():
        pass_two(0, 0).start()

    def cross_own():
        ma_wait(0, 0)
        ms(0).start()

    gather(f)
    a_pool[y, c, :, lanes(f)] = a_send[f]
    loop(0, 2, lambda i: ma(0, 1 + 2 * i).start())
    loop(1, 16, block)
    comm("wx", 0, 2, wx, False)
    waits["m1_s"] = lambda: loop(1, 16, lambda r: m1(r).wait_send())
    loop(16 - LAG, 16, pass_on)
    waits["ma_s"] = lambda: loop(0, 16, lambda r: loop(1, 4, lambda i: ma(r, i).wait_send()))
    loop(16 - LAG_F, 16, forward)
    loop(16 - LAG_C, 16, cross)
    waits["ms_s"] = lambda: loop(0, 16, lambda r: ms(r).wait_send())

    def ms_all():
        send(a_pool.at[:, c], a_pool.at[:, c], ms_s.at[0], ms_r.at[0], dp=sibling).wait_recv()

    waits["ms_r"] = ms_all
    now("wx_r")
    now("ms_r")

    def hm(r):
        to_y, to_c = yc_at(r)
        return send(
            h_send.at[to_y, to_c], hidden_vmem.at[:, lanes(y * 2 + c)], h_s.at[r], h_r.at[r],
            dp=to_y * 4 + xh * 2 + to_c,
        )

    for q in (2, 1, 3, 0):
        to_y = (y + q) % 4
        out = jnp.dot(
            a_pool[to_y].reshape(2 * ROWS, 2048), w1[...].reshape(2048, 128), preferred_element_type=F32
        )
        pre[to_y] = out.reshape(2, ROWS, 128)
        h_send[to_y] = (out * sigmoid(out)).astype(BF16).reshape(2, ROWS, 128)
        for r in (2 * q, 2 * q + 1):
            if r:
                hm(r).start()
    comm("hm", 1, 8, hm, False)
    hidden_vmem[:, lanes(y * 2 + c)] = h_send[y, c]
    now("hm_r")
    hidden_out = pltpu.make_async_copy(hidden_vmem, hidden_ref, load_sem.at[14])
    hidden_out.start()
    waits["hidden"] = lambda: hidden_out.wait()

    eye = lax.broadcasted_iota(jnp.int32, (SEEDS, SEEDS), 0) == lax.broadcasted_iota(jnp.int32, (SEEDS, SEEDS), 1)

    def column(row):
        return jnp.sum(jnp.where(eye, row, 0), axis=1, keepdims=True)

    counts = column(cnt_ref[...])
    count_float = counts.astype(F32)
    col = lax.broadcasted_iota(jnp.int32, (SEEDS, ROWS), 1)
    table = jnp.zeros((SEEDS, ROWS), F32)
    for j in range(FAN2):
        table = table + jnp.where((column(nbr_ref[j]) == col) & (j < counts), 1.0, 0.0)
    hidden = hidden_vmem[...]
    seed_hidden = hidden[:SEEDS]
    neigh = (jnp.dot(table.astype(BF16), hidden, preferred_element_type=F32) / count_float).astype(BF16)

    wide_left = lax.broadcasted_iota(jnp.int32, (SEEDS, 128), 1) < 64
    for hx in range(2):
        for q in range(4):
            lo = hx * 512 + q * 128
            s = seed_hidden[:, lo:lo + 128].astype(F32)
            n = neigh[:, lo:lo + 128].astype(F32)
            here = slice(hx * 128, hx * 128 + 128)
            sn_send[2 * q, :, here] = jnp.where(wide_left, s, pltpu.roll(n, 64, 1)).astype(BF16)
            sn_send[2 * q + 1, :, here] = jnp.where(wide_left, pltpu.roll(s, 64, 1), n).astype(BF16)

    def sz(r):
        return send(sn_send.at[(z + r) % 8], sn_pool.at[z, y, c], sz_s.at[r], sz_r.at[r], feat=z_at(r))

    comm("sz", 1, 8, sz)
    sn_pool[z, y, c] = sn_send[z]

    now("w2")
    both = jnp.concatenate([seed_hidden, neigh], axis=1)
    upper_pre = jnp.dot(both, w2[...], preferred_element_type=F32)
    upper_sigma = sigmoid(upper_pre)
    upper_hidden = (upper_pre * upper_sigma).astype(BF16)
    logits = lax.dot_general(upper_hidden, headp[...], NT, preferred_element_type=F32)
    logits_ref[...] = logits[:, 0:CLASSES]
    cls = lax.broadcasted_iota(jnp.int32, (SEEDS, 128), 1)
    live = cls < CLASSES
    top = jnp.max(jnp.where(live, logits, -jnp.inf), axis=1, keepdims=True)
    expo = jnp.where(live, jnp.exp(jnp.where(live, logits - top, 0.0)), 0.0)
    probability = expo / jnp.sum(expo, axis=1, keepdims=True)
    one_hot = jnp.where(cls == column(lab_ref[...]), 1.0, 0.0)
    grad_logits = ((probability - one_hot) / 256.0).astype(BF16)

    for hx in range(2):
        for q in range(4):
            lo = hx * 512 + q * 128
            p_send[hx, q, :, 0:128] = upper_hidden[:, lo:lo + 128]
            p_send[hx, q, :, 128:256] = grad_logits

    def m2(r):
        to = feat_at(r)
        return send(p_send.at[to // 8, (to % 8) // 2], p_recv.at[f], m2_s.at[r], m2_r.at[r], feat=to)

    comm("m2", 1, 16, m2)
    p_recv[f] = p_send[xl, quad]

    back_hidden = jnp.dot(grad_logits, headp[...], preferred_element_type=F32)
    slope_two = upper_sigma + upper_pre * upper_sigma * (1.0 - upper_sigma)
    grad_upper = (back_hidden * slope_two).astype(BF16)
    back_two = lax.dot_general(grad_upper, w2[...], NT, preferred_element_type=F32)
    back = jnp.concatenate([back_two[:, 0:WIDE], back_two[:, WIDE:2 * WIDE] / count_float], axis=0)
    back = jnp.concatenate([back.astype(BF16), grad_upper], axis=0)
    wide_table = jnp.concatenate([table, jnp.zeros((SEEDS, 128 - ROWS), F32)], axis=1).astype(BF16)
    for e in range(8):
        b_send[e // 2, e % 2, 0:3 * SEEDS] = back[:, e * 128:e * 128 + 128]
        b_send[e // 2, e % 2, 3 * SEEDS:4 * SEEDS] = wide_table

    def m3(r):
        to_y, to_c = yc_at(r)
        return send(
            b_send.at[to_y, to_c], b_pool.at[y, c], m3_s.at[r], m3_r.at[r], dp=to_y * 4 + xh * 2 + to_c
        )

    comm("m3", 1, 8, m3)
    b_pool[y, c] = b_send[y, c]

    first = jnp.where(lax.broadcasted_iota(jnp.int32, (SEEDS, ROWS), 0) == col, 1.0, 0.0).astype(BF16)
    for r in range(8):
        if r:
            m3(r).wait_recv()
        at_y, at_c = (y + 4 - r // 2) % 4, (c + r) % 2
        terms = b_pool[at_y, at_c]
        spread = jnp.concatenate([first, terms[3 * SEEDS:4 * SEEDS, 0:ROWS]], axis=0)
        rows_back = lax.dot_general(spread, terms[0:2 * SEEDS], TN, preferred_element_type=F32)
        g_pool[at_y, at_c] = (rows_back * silu_slope(pre[at_y, at_c])).astype(BF16)
    waits.pop("m3_r")
    gu_all[z] = b_pool[:, :, 2 * SEEDS:3 * SEEDS]

    def gz(r):
        return send(gu_all.at[z], gu_all.at[z], gz_s.at[r], gz_r.at[r], feat=z_at(r))

    comm("gz", 1, 8, gz)

    g_turned[...] = g_pool[...].reshape(8 * ROWS, 128).T

    def to_final(n, src, dst, ss, rs):
        to_l, to_c = (xl + n // 2) % 2, (c + n % 2) % 2
        return send(src(to_c, to_l), dst(x), ss.at[n], rs.at[x], feat=to_l * 8 + z, dp=y * 4 + c * 2 + to_c)

    def final_start(src, dst, ss, rs):
        pl.when(xh != c)(lambda: to_final(0, src, dst, ss, rs).start())
        loop(1, 4, lambda n: to_final(n, src, dst, ss, rs).start())

        @pl.when(xh == c)
        def _():
            dst(x)[...] = src(c, xl)[...]

    def final_sent(src, dst, ss, rs):
        pl.when(xh != c)(lambda: to_final(0, src, dst, ss, rs).wait_send())
        loop(1, 4, lambda n: to_final(n, src, dst, ss, rs).wait_send())

    def final_came(src, dst, ss, rs):
        def came(n):
            @pl.when(jnp.logical_not((xh == c) & (n == x)))
            def _():
                send(src(0, 0), dst(n), ss.at[1], rs.at[n], feat=f, dp=d).wait_recv()

        loop(0, 4, came)

    def order(i):
        return 4 + (i // 2) * (1 - i % 2) - ((i + 1) // 2) * (i % 2)

    def x1(r):
        to_z = (z + r) % 8
        return (
            lambda to_c, to_l: x1_send.at[to_c, to_l, to_z],
            lambda n: x1_recv.at[n, to_z],
            x1_s.at[r],
            x1_r.at[r],
        )

    for i in range(8):
        to_z = (z + order(i)) % 8
        right = jnp.concatenate(
            [a_pool[:, :, :, lanes(to_z)].reshape(8 * ROWS, 128), a_pool[:, :, :, lanes(8 + to_z)].reshape(8 * ROWS, 128)],
            axis=1,
        )
        out = jnp.dot(g_turned[...], right, preferred_element_type=F32).astype(BF16)
        for to_c in range(2):
            for to_l in range(2):
                x1_send[to_c, to_l, to_z] = out[to_c * 64:to_c * 64 + 64, to_l * 128:to_l * 128 + 128]
        final_start(*x1(order(i)))
    waits["x1_s"] = lambda: loop(0, 8, lambda r: final_sent(*x1(r)))

    def sy(r):
        spot = sn_pool.at[:, y, c]
        return send(spot, spot, sy_s.at[r], sy_r.at[r], dp=y_at(r))

    def sc(n):
        spot = sn_pool.at[:, :, c]
        return send(spot, spot, sc_s.at[n], sc_r.at[n], dp=sibling)

    now("sz_r")
    comm("sy", 1, 4, sy)

    now("m2_r")
    every = p_recv[...].reshape(16 * SEEDS, 256)
    head_part = lax.dot_general(every[:, 128:256], every[:, 0:128], TN, preferred_element_type=F32)
    hd_send[...] = head_part[0:32].astype(BF16)

    def m5(r):
        return send(hd_send, hd_recv.at[d], m5_s.at[r], m5_r.at[r], dp=(d + r) % 16)

    comm("m5", 1, 16, m5)
    hd_recv[d] = hd_send[...]

    def z1(r):
        return send(z1_send.at[r], z1_recv.at[z], z1_s.at[r], z1_r.at[r], feat=z_at(r))

    def z1_start(i):
        r = order(i)
        final_came(*x1(r))
        z1_send[r] = jnp.sum(x1_recv[:, (z + r) % 8].astype(F32), axis=0).astype(BF16)
        pl.when(i < 7)(lambda: z1(r).start())

    loop(0, 8, z1_start)
    comm("z1", 1, 8, z1, False)
    z1_recv[z] = z1_send[0]

    now("sy_r")
    comm("sc", 0, 1, sc)
    now("gz_r")
    now("sc_r")
    part_two = lax.dot_general(
        gu_all[...].reshape(64 * SEEDS, 128), sn_pool[...].reshape(64 * SEEDS, 256), TN, preferred_element_type=F32
    ).astype(BF16)
    for to_c in range(2):
        for to_l in range(2):
            x2_send[to_c, to_l] = part_two[to_c * 64:to_c * 64 + 64, to_l * 128:to_l * 128 + 128]

    x2 = (lambda to_c, to_l: x2_send.at[to_c, to_l], lambda n: x2_recv.at[n], x2_s, x2_r)
    final_start(*x2)
    waits["x2_s"] = lambda: final_sent(*x2)
    waits["x2_r"] = lambda: final_came(*x2)

    now("m5_r")
    head_sum = jnp.sum(hd_recv[...].astype(F32), axis=0)
    head_sum = jnp.where(f % 2 == 1, pltpu.roll(head_sum, 64, 1), head_sum)
    ghead_ref[...] = head_sum[0:CLASSES, 0:64]

    now("x2_r")
    two_ref[...] = jnp.sum(x2_recv[...].astype(F32), axis=0).T.reshape(2, 64, 64)
    now("z1_r")
    one_ref[...] = jnp.sum(z1_recv[...].astype(F32), axis=0).T.reshape(2, 64, 64)

    for wait in waits.values():
        wait()


def finish(*refs):
    for i in range(5):
        refs[5 + i][...] = refs[i][...]


def shards(
    node_feats, target_ids, layer_one_nbrs, layer_one_counts, layer_two_nbrs, layer_two_counts, labels,
    layer_one_weight, layer_two_weight, head_weight,
):
    vmem = pl.BlockSpec(memory_space=pltpu.VMEM)
    smem = pl.BlockSpec(memory_space=pltpu.SMEM)
    hbm = pl.BlockSpec(memory_space=pltpu.HBM)
    dma = pltpu.SemaphoreType.DMA
    results = pl.pallas_call(
        kernel,
        out_shape=(
            jax.ShapeDtypeStruct((ROWS, WIDE), BF16),
            jax.ShapeDtypeStruct((SEEDS, CLASSES), F32),
            jax.ShapeDtypeStruct((2, 64, 64), F32),
            jax.ShapeDtypeStruct((2, 64, 64), F32),
            jax.ShapeDtypeStruct((CLASSES, 64), F32),
        ),
        in_specs=[smem, vmem, vmem, hbm, hbm, hbm, vmem, vmem, vmem, vmem],
        out_specs=(hbm, vmem, vmem, vmem, vmem),
        scratch_shapes=[
            pltpu.VMEM((1, FAN1 * TARGETS), jnp.int32),
            pltpu.SMEM((1, FAN1 * TARGETS), jnp.int32),
            pltpu.VMEM((1, TARGETS), F32),
            pltpu.SMEM((1, TARGETS), F32),
            pltpu.VMEM((64, NODES), BF16),
            pltpu.VMEM((NODES + 8, 128), F32),
            pltpu.VMEM((ROWS, 128), F32),
            pltpu.VMEM((16, ROWS, 128), BF16),
            pltpu.VMEM((4, 2, ROWS, 2048), BF16),
            pltpu.VMEM((2, 8, 128, 128), BF16),
            pltpu.VMEM((2 * WIDE, WIDE), BF16),
            pltpu.VMEM((128, WIDE), BF16),
            pltpu.VMEM((4, 2, ROWS, 128), F32),
            pltpu.VMEM((4, 2, ROWS, 128), BF16),
            pltpu.VMEM((ROWS, WIDE), BF16),
            pltpu.VMEM((2, 4, SEEDS, 256), BF16),
            pltpu.VMEM((16, SEEDS, 256), BF16),
            pltpu.VMEM((8, SEEDS, 256), BF16),
            pltpu.VMEM((8, 4, 2, SEEDS, 256), BF16),
            pltpu.VMEM((4, 2, 4 * SEEDS, 128), BF16),
            pltpu.VMEM((4, 2, 4 * SEEDS, 128), BF16),
            pltpu.VMEM((4, 2, ROWS, 128), BF16),
            pltpu.VMEM((8, 4, 2, SEEDS, 128), BF16),
            pltpu.VMEM((128, 8 * ROWS), BF16),
            pltpu.VMEM((2, 2, 8, 64, 128), BF16),
            pltpu.VMEM((4, 8, 64, 128), BF16),
            pltpu.VMEM((8, 64, 128), BF16),
            pltpu.VMEM((8, 64, 128), BF16),
            pltpu.VMEM((2, 2, 64, 128), BF16),
            pltpu.VMEM((4, 64, 128), BF16),
            pltpu.VMEM((32, 128), BF16),
            pltpu.VMEM((16, 32, 128), BF16),
            dma((15,)),
            dma((8,)), dma((8,)),
            dma((2,)), dma((2,)),
            dma((16,)), dma((16,)),
            dma((16, 4)), dma((16, 4)),
            dma((16,)), dma((1,)),
            dma((8,)), dma((8,)),
            dma((16,)), dma((16,)),
            dma((8,)), dma((8,)),
            dma((4,)), dma((4,)),
            dma((1,)), dma((1,)),
            dma((8,)), dma((8,)),
            dma((8,)), dma((8,)),
            dma((8, 4)), dma((8, 4)),
            dma((8,)), dma((8,)),
            dma((4,)), dma((4,)),
            dma((16,)), dma((16,)),
        ],
        compiler_params=pltpu.CompilerParams(
            collective_id=0, has_side_effects=True, vmem_limit_bytes=60 * 1024 * 1024
        ),
        name="step",
    )(
        target_ids, layer_one_nbrs.transpose(2, 0, 1), layer_one_counts, node_feats[0].T,
        layer_one_weight.reshape(128, WIDE), layer_two_weight.reshape(2 * WIDE, WIDE), head_weight.T,
        layer_two_nbrs.transpose(2, 0, 1), layer_two_counts, labels,
    )
    hidden, logits, grad_one, grad_two, grad_head = pl.pallas_call(
        finish,
        out_shape=tuple(jax.ShapeDtypeStruct(r.shape, r.dtype) for r in results),
        in_specs=[vmem] * 5,
        out_specs=(vmem,) * 5,
        name="finish",
    )(*results)
    return hidden[None], logits[None], grad_one, grad_two, grad_head.T


def solution(mesh):
    return jax.shard_map(
        shards,
        mesh=mesh,
        in_specs=(
            P("dp", None, "feat"),
            P("dp", None),
            P("dp", None, None),
            P("dp", None),
            P("dp", "feat", None),
            P("dp", "feat"),
            P("dp", "feat"),
            P(None, "feat", None),
            P(),
            P(),
        ),
        out_specs=(
            P("dp", "feat", None),
            P("dp", "feat", None),
            P(None, "feat", "dp"),
            P(None, "feat", "dp"),
            P("feat", None),
        ),
        check_vma=False,
    )
```

```python
import functools

import jax
import jax.numpy as jnp
from jax import lax
from jax.experimental import pallas as pl
from jax.experimental.pallas import tpu as pltpu
from jax.sharding import PartitionSpec as P

MESH = pl.DeviceIdType.MESH
BF16 = jnp.bfloat16
F32 = jnp.float32

NODES = 6144
ROWS = 96
TARGETS = 16 * ROWS
UNROLL = 16
SEEDS = 16
FAN1 = 10
FAN2 = 5
CLASSES = 19
WIDE = 1024
SEQUENCE = (0, 8, 1, 7, 2, 6, 3, 5, 4, 12, 11, 13, 10, 14, 9, 15)
DIRECT = (9, 15)
TRAVEL = {0: 3.0, 1: 6.0, 2: 6.5, 3: 7.5, 4: 8.0}
HOP = 3.0
WX_STEP = 12.0
TN = (((0,), (0,)), ((), ()))
NT = (((1,), (1,)), ((), ()))


def sigmoid(values):
    return 1.0 / (1.0 + jnp.exp(-values))


def silu_slope(values):
    sigma = sigmoid(values)
    return sigma + values * sigma * (1.0 - sigma)


def kernel(
    self_ref, one_nbr_ref, one_cnt_ref, feats_hbm, w1_hbm, w2_hbm, head_ref, nbr_ref, cnt_ref, lab_ref,
    hidden_ref, logits_ref, one_ref, two_ref, ghead_ref,
    idx_vmem, idx_ref, inv_vmem, inv_ref, feats, tab, rows, a_send, a_pool, w1, w2, headp, pre, h_send, hidden_vmem,
    p_send, p_recv, sn_send, sn_pool, b_send, b_pool, g_pool, gu_all, g_turned,
    x1_send, x1_recv, z1_send, z1_recv, x2_send, x2_recv, hd_send, hd_recv,
    load_sem, wa_s, wa_r, wx_s, wx_r, m1_s, m1_r, ma_s, ma_r, ms_s, ms_r, h_s, h_r, m2_s, m2_r,
    sz_s, sz_r, sy_s, sy_r, sc_s, sc_r, m3_s, m3_r, gz_s, gz_r, x1_s, x1_r, z1_s, z1_r, x2_s, x2_r, m5_s, m5_r,
):
    f = lax.axis_index("feat")
    d = lax.axis_index("dp")
    xl, z = f // 8, f % 8
    y, xh, c = d // 4, (d // 2) % 2, d % 2
    x = xh * 2 + xl
    quad = z // 2

    def feat_at(r):
        return ((xl + r // 8) % 2) * 8 + (z + r % 8) % 8

    def feat_from(r):
        return ((xl + r // 8) % 2) * 8 + (z + 8 - r % 8) % 8

    def z_at(r):
        return xl * 8 + (z + r) % 8

    def y_at(r):
        return ((y + r) % 4) * 4 + xh * 2 + c

    def x_at(r):
        to = (x + r) % 4
        return {"feat": (to % 2) * 8 + z, "dp": y * 4 + (to // 2) * 2 + c}

    def yc_at(r):
        return (y + r // 2) % 4, (c + r % 2) % 2

    sibling = y * 4 + xh * 2 + 1 - c

    def send(src, dst, ss, rs, **where):
        return pltpu.make_async_remote_copy(
            src_ref=src, dst_ref=dst, send_sem=ss, recv_sem=rs, device_id=where, device_id_type=MESH
        )

    def loop(lo, hi, fn):
        def body(i, carry):
            fn(i)
            return carry

        lax.fori_loop(lo, hi, body, 0)

    def lanes(block):
        return pl.ds(pl.multiple_of(block * 128, 128), 128)

    waits = {}

    def now(name):
        waits.pop(name)()

    def comm(name, lo, hi, make, start=True):
        if start:
            loop(lo, hi, lambda r: make(r).start())
        waits[name + "_s"] = lambda: loop(lo, hi, lambda r: make(r).wait_send())
        waits[name + "_r"] = lambda: loop(lo, hi, lambda r: make(r).wait_recv())

    barrier = pltpu.get_barrier_semaphore()

    def greet(r):
        pl.semaphore_signal(barrier, inc=1, device_id={"feat": feat_at(r)}, device_id_type=MESH)
        pl.semaphore_signal(barrier, inc=1, device_id={"dp": (d + r) % 16}, device_id_type=MESH)

    loop(1, 16, greet)
    for n in range(1, 4):
        corner = {"feat": (1 - xl) * 8 + z, "dp": y * 4 + ((xh + n // 2) % 2) * 2 + (c + n % 2) % 2}
        pl.semaphore_signal(barrier, inc=1, device_id=corner, device_id_type=MESH)

    w1_load = pltpu.make_async_copy(w1_hbm.at[:, lanes(y * 2 + c)], w1.at[xl, z], load_sem.at[2])
    w1_load.start()
    waits["w1"] = lambda: w1_load.wait()

    def feat_load(i):
        part = pl.ds(pl.multiple_of(i * 1024, 1024), 1024)
        return pltpu.make_async_copy(feats_hbm.at[:, part], feats.at[:, part], load_sem.at[4 + i])

    loop(0, 6, lambda i: feat_load(i).start())
    waits["feats"] = lambda: loop(0, 6, lambda i: feat_load(i).wait())
    w2_load = pltpu.make_async_copy(w2_hbm, w2, load_sem.at[1])
    w2_load.start()
    waits["w2"] = lambda: w2_load.wait()

    one_counts = one_cnt_ref[...]
    for j in range(FAN1):
        idx_vmem[:, j * TARGETS:(j + 1) * TARGETS] = jnp.where(j < one_counts, one_nbr_ref[j], NODES)
    inv_vmem[...] = 1.0 / one_counts.astype(F32)
    idx_load = pltpu.make_async_copy(idx_vmem, idx_ref, load_sem.at[0])
    idx_load.start()
    waits["idx"] = lambda: idx_load.wait()
    inv_load = pltpu.make_async_copy(inv_vmem, inv_ref, load_sem.at[3])
    inv_load.start()
    waits["inv"] = lambda: inv_load.wait()
    headp[...] = jnp.zeros_like(headp)
    headp[0:CLASSES, :] = head_ref[...]

    def wa(r):
        return send(w1.at[xl, z], w1.at[xl, z], wa_s.at[r], wa_r.at[r], feat=z_at(r))

    def wx(n):
        spot = w1.at[xl, pl.ds(xh * 4, 4)]
        return send(spot, spot, wx_s.at[n], wx_r.at[n], **x_at(1 + 2 * n))

    now("w1")
    pl.semaphore_wait(barrier, 33)
    comm("wa", 1, 8, wa)

    waits.pop("feats")

    for i in range(6):
        feat_load(i).wait()
        for first in range(i * 1024, i * 1024 + 1024, 128):
            part = feats[:, first:first + 128]
            tab[first:first + 128, :] = jnp.concatenate([part, part], axis=0).T.astype(F32)
    tab[pl.ds(NODES, 8), :] = jnp.zeros((8, 128), F32)
    now("idx")
    now("inv")

    lane = lax.broadcasted_iota(jnp.int32, (1, 128), 1)
    left = lane < 64

    def gather(k):
        def body(g):
            for u in range(UNROLL):
                local = g * UNROLL + u
                t = k * ROWS + local
                own = tab[pl.ds(self_ref[0, t], 1), :]
                total = [tab[pl.ds(idx_ref[0, j * TARGETS + t], 1), :] for j in range(FAN1)]
                while len(total) > 1:
                    total = [
                        total[i] + total[i + 1] if i + 1 < len(total) else total[i]
                        for i in range(0, len(total), 2)
                    ]
                rows[pl.ds(local, 1), :] = jnp.where(left, own, total[0] * inv_ref[0, t])

        loop(0, ROWS // UNROLL, body)
        a_send[k] = rows[...].astype(BF16)

    def m1(r):
        return send(a_send.at[feat_at(r)], a_pool.at[f, y, c], m1_s.at[r], m1_r.at[r], feat=feat_at(r))

    def ma(r, i):
        spot = a_pool.at[feat_from(r), y, c]
        return send(spot, spot, ma_s.at[r, i], ma_r.at[r, i], dp=y_at(i))

    def ma_two(place, r):
        after = 1 + 2 * (place % 2)
        spot = a_pool.at[feat_from(r), (y + 4 - after) % 4, c]
        return send(spot, spot, ma_s.at[r, 2], ma_r.at[r, 2], dp=y_at(after))

    def ms(r):
        spot = a_pool.at[feat_from(r), :, c]
        return send(spot, spot, ms_s.at[r], ms_r.at[0], dp=sibling)

    def pass_on(place, r):
        if r:
            m1(r).wait_recv()
        for i in (1, 2, 3) if r in DIRECT else (1, 3):
            ma(r, i).start()

    def forward(place, r):
        ma(r, 1 + 2 * (place % 2)).wait_recv()
        ma_two(place, r).start()

    def cross(place, r):
        for i in (1, 2, 3) if r in DIRECT else (2, 3 - 2 * (place % 2)):
            ma(r, i).wait_recv()
        ms(r).start()

    def wx_start(place, r):
        now("wa_r")
        loop(0, 2, lambda n: wx(n).start())

    events = [(WX_STEP, wx_start, 0, 0)]
    for place, r in enumerate(SEQUENCE):
        at = place + 1 + (TRAVEL[min(r % 8, 8 - r % 8)] if r else 0.0)
        events.append((at, pass_on, place, r))
        if r not in DIRECT:
            at += HOP
            events.append((at, forward, place, r))
        events.append((at + HOP, cross, place, r))
    events.sort(key=lambda event: event[0])

    def run_events(until):
        while events and events[0][0] <= until:
            _, act, place, r = events.pop(0)
            act(place, r)

    for place, r in enumerate(SEQUENCE):
        gather(feat_at(r))
        if r:
            m1(r).start()
        else:
            a_pool[f, y, c] = a_send[f]
        run_events(place + 1)
    run_events(1000)
    comm("wx", 0, 2, wx, False)
    waits["m1_s"] = lambda: loop(1, 16, lambda r: m1(r).wait_send())
    waits["ma_s"] = lambda: loop(0, 16, lambda r: loop(1, 4, lambda i: ma(r, i).wait_send()))
    waits["ms_s"] = lambda: loop(0, 16, lambda r: ms(r).wait_send())

    def ms_all():
        send(a_pool.at[:, :, c], a_pool.at[:, :, c], ms_s.at[0], ms_r.at[0], dp=sibling).wait_recv()

    waits["ms_r"] = ms_all
    now("wx_r")
    now("ms_r")

    def hm(r):
        to_y, to_c = yc_at(r)
        return send(
            h_send.at[to_y, to_c], hidden_vmem.at[:, lanes(y * 2 + c)], h_s.at[r], h_r.at[r],
            dp=to_y * 4 + xh * 2 + to_c,
        )

    for q in (2, 1, 3, 0):
        to_y = (y + q) % 4
        wide = jnp.concatenate([a_pool[b, to_y].reshape(2 * ROWS, 128) for b in range(16)], axis=1)
        out = jnp.dot(wide, w1[...].reshape(2048, 128), preferred_element_type=F32)
        pre[to_y] = out.reshape(2, ROWS, 128)
        h_send[to_y] = (out * sigmoid(out)).astype(BF16).reshape(2, ROWS, 128)
        for r in (2 * q, 2 * q + 1):
            if r:
                hm(r).start()
    comm("hm", 1, 8, hm, False)
    hidden_vmem[:, lanes(y * 2 + c)] = h_send[y, c]
    now("hm_r")
    hidden_out = pltpu.make_async_copy(hidden_vmem, hidden_ref, load_sem.at[14])
    hidden_out.start()
    waits["hidden"] = lambda: hidden_out.wait()

    eye = lax.broadcasted_iota(jnp.int32, (SEEDS, SEEDS), 0) == lax.broadcasted_iota(jnp.int32, (SEEDS, SEEDS), 1)

    def column(row):
        return jnp.sum(jnp.where(eye, row, 0), axis=1, keepdims=True)

    counts = column(cnt_ref[...])
    count_float = counts.astype(F32)
    col = lax.broadcasted_iota(jnp.int32, (SEEDS, ROWS), 1)
    table = jnp.zeros((SEEDS, ROWS), F32)
    for j in range(FAN2):
        table = table + jnp.where((column(nbr_ref[j]) == col) & (j < counts), 1.0, 0.0)
    hidden = hidden_vmem[...]
    seed_hidden = hidden[:SEEDS]
    neigh = (jnp.dot(table.astype(BF16), hidden, preferred_element_type=F32) / count_float).astype(BF16)

    wide_left = lax.broadcasted_iota(jnp.int32, (SEEDS, 128), 1) < 64
    for hx in range(2):
        for q in range(4):
            lo = hx * 512 + q * 128
            s = seed_hidden[:, lo:lo + 128].astype(F32)
            n = neigh[:, lo:lo + 128].astype(F32)
            here = slice(hx * 128, hx * 128 + 128)
            sn_send[2 * q, :, here] = jnp.where(wide_left, s, pltpu.roll(n, 64, 1)).astype(BF16)
            sn_send[2 * q + 1, :, here] = jnp.where(wide_left, pltpu.roll(s, 64, 1), n).astype(BF16)

    def sz(r):
        return send(sn_send.at[(z + r) % 8], sn_pool.at[z, y, c], sz_s.at[r], sz_r.at[r], feat=z_at(r))

    comm("sz", 1, 8, sz)
    sn_pool[z, y, c] = sn_send[z]

    now("w2")
    both = jnp.concatenate([seed_hidden, neigh], axis=1)
    upper_pre = jnp.dot(both, w2[...], preferred_element_type=F32)
    upper_sigma = sigmoid(upper_pre)
    upper_hidden = (upper_pre * upper_sigma).astype(BF16)
    logits = lax.dot_general(upper_hidden, headp[...], NT, preferred_element_type=F32)
    logits_ref[...] = logits[:, 0:CLASSES]
    cls = lax.broadcasted_iota(jnp.int32, (SEEDS, 128), 1)
    live = cls < CLASSES
    top = jnp.max(jnp.where(live, logits, -jnp.inf), axis=1, keepdims=True)
    expo = jnp.where(live, jnp.exp(jnp.where(live, logits - top, 0.0)), 0.0)
    probability = expo / jnp.sum(expo, axis=1, keepdims=True)
    one_hot = jnp.where(cls == column(lab_ref[...]), 1.0, 0.0)
    grad_logits = ((probability - one_hot) / 256.0).astype(BF16)

    for hx in range(2):
        for q in range(4):
            lo = hx * 512 + q * 128
            p_send[hx, q, :, 0:128] = upper_hidden[:, lo:lo + 128]
            p_send[hx, q, :, 128:256] = grad_logits

    def m2(r):
        to = feat_at(r)
        return send(p_send.at[to // 8, (to % 8) // 2], p_recv.at[f], m2_s.at[r], m2_r.at[r], feat=to)

    comm("m2", 1, 16, m2)
    p_recv[f] = p_send[xl, quad]

    back_hidden = jnp.dot(grad_logits, headp[...], preferred_element_type=F32)
    slope_two = upper_sigma + upper_pre * upper_sigma * (1.0 - upper_sigma)
    grad_upper = (back_hidden * slope_two).astype(BF16)
    back_two = lax.dot_general(grad_upper, w2[...], NT, preferred_element_type=F32)
    back = jnp.concatenate([back_two[:, 0:WIDE], back_two[:, WIDE:2 * WIDE] / count_float], axis=0)
    back = jnp.concatenate([back.astype(BF16), grad_upper], axis=0)
    wide_table = jnp.concatenate([table, jnp.zeros((SEEDS, 128 - ROWS), F32)], axis=1).astype(BF16)
    for e in range(8):
        b_send[e // 2, e % 2, 0:3 * SEEDS] = back[:, e * 128:e * 128 + 128]
        b_send[e // 2, e % 2, 3 * SEEDS:4 * SEEDS] = wide_table

    def m3(r):
        to_y, to_c = yc_at(r)
        return send(
            b_send.at[to_y, to_c], b_pool.at[y, c], m3_s.at[r], m3_r.at[r], dp=to_y * 4 + xh * 2 + to_c
        )

    comm("m3", 1, 8, m3)
    b_pool[y, c] = b_send[y, c]

    first = jnp.where(lax.broadcasted_iota(jnp.int32, (SEEDS, ROWS), 0) == col, 1.0, 0.0).astype(BF16)
    for r in range(8):
        if r:
            m3(r).wait_recv()
        at_y, at_c = (y + 4 - r // 2) % 4, (c + r) % 2
        terms = b_pool[at_y, at_c]
        spread = jnp.concatenate([first, terms[3 * SEEDS:4 * SEEDS, 0:ROWS]], axis=0)
        rows_back = lax.dot_general(spread, terms[0:2 * SEEDS], TN, preferred_element_type=F32)
        g_pool[at_y, at_c] = (rows_back * silu_slope(pre[at_y, at_c])).astype(BF16)
    waits.pop("m3_r")
    gu_all[z] = b_pool[:, :, 2 * SEEDS:3 * SEEDS]

    def gz(r):
        return send(gu_all.at[z], gu_all.at[z], gz_s.at[r], gz_r.at[r], feat=z_at(r))

    comm("gz", 1, 8, gz)

    g_turned[...] = g_pool[...].reshape(8 * ROWS, 128).T

    def to_final(n, src, dst, ss, rs):
        to_l, to_c = (xl + n // 2) % 2, (c + n % 2) % 2
        return send(src(to_c, to_l), dst(x), ss.at[n], rs.at[x], feat=to_l * 8 + z, dp=y * 4 + c * 2 + to_c)

    def final_start(src, dst, ss, rs):
        pl.when(xh != c)(lambda: to_final(0, src, dst, ss, rs).start())
        loop(1, 4, lambda n: to_final(n, src, dst, ss, rs).start())

        @pl.when(xh == c)
        def _():
            dst(x)[...] = src(c, xl)[...]

    def final_sent(src, dst, ss, rs):
        pl.when(xh != c)(lambda: to_final(0, src, dst, ss, rs).wait_send())
        loop(1, 4, lambda n: to_final(n, src, dst, ss, rs).wait_send())

    def final_came(src, dst, ss, rs):
        def came(n):
            @pl.when(jnp.logical_not((xh == c) & (n == x)))
            def _():
                send(src(0, 0), dst(n), ss.at[1], rs.at[n], feat=f, dp=d).wait_recv()

        loop(0, 4, came)

    def order(i):
        return 4 + (i // 2) * (1 - i % 2) - ((i + 1) // 2) * (i % 2)

    def x1(r):
        to_z = (z + r) % 8
        return (
            lambda to_c, to_l: x1_send.at[to_c, to_l, to_z],
            lambda n: x1_recv.at[n, to_z],
            x1_s.at[r],
            x1_r.at[r],
        )

    for i in range(8):
        to_z = (z + order(i)) % 8
        right = jnp.concatenate(
            [a_pool[to_z].reshape(8 * ROWS, 128), a_pool[8 + to_z].reshape(8 * ROWS, 128)],
            axis=1,
        )
        out = jnp.dot(g_turned[...], right, preferred_element_type=F32).astype(BF16)
        for to_c in range(2):
            for to_l in range(2):
                x1_send[to_c, to_l, to_z] = out[to_c * 64:to_c * 64 + 64, to_l * 128:to_l * 128 + 128]
        final_start(*x1(order(i)))
    waits["x1_s"] = lambda: loop(0, 8, lambda r: final_sent(*x1(r)))

    def sy(r):
        spot = sn_pool.at[:, y, c]
        return send(spot, spot, sy_s.at[r], sy_r.at[r], dp=y_at(r))

    def sc(n):
        spot = sn_pool.at[:, :, c]
        return send(spot, spot, sc_s.at[n], sc_r.at[n], dp=sibling)

    now("sz_r")
    comm("sy", 1, 4, sy)

    now("m2_r")
    every = p_recv[...].reshape(16 * SEEDS, 256)
    head_part = lax.dot_general(every[:, 128:256], every[:, 0:128], TN, preferred_element_type=F32)
    hd_send[...] = head_part[0:32].astype(BF16)

    def m5(r):
        return send(hd_send, hd_recv.at[d], m5_s.at[r], m5_r.at[r], dp=(d + r) % 16)

    comm("m5", 1, 16, m5)
    hd_recv[d] = hd_send[...]

    def z1(r):
        return send(z1_send.at[r], z1_recv.at[z], z1_s.at[r], z1_r.at[r], feat=z_at(r))

    def z1_start(i):
        r = order(i)
        final_came(*x1(r))
        z1_send[r] = jnp.sum(x1_recv[:, (z + r) % 8].astype(F32), axis=0).astype(BF16)
        pl.when(i < 7)(lambda: z1(r).start())

    loop(0, 8, z1_start)
    comm("z1", 1, 8, z1, False)
    z1_recv[z] = z1_send[0]

    now("sy_r")
    comm("sc", 0, 1, sc)
    now("gz_r")
    now("sc_r")
    part_two = lax.dot_general(
        gu_all[...].reshape(64 * SEEDS, 128), sn_pool[...].reshape(64 * SEEDS, 256), TN, preferred_element_type=F32
    ).astype(BF16)
    for to_c in range(2):
        for to_l in range(2):
            x2_send[to_c, to_l] = part_two[to_c * 64:to_c * 64 + 64, to_l * 128:to_l * 128 + 128]

    x2 = (lambda to_c, to_l: x2_send.at[to_c, to_l], lambda n: x2_recv.at[n], x2_s, x2_r)
    final_start(*x2)
    waits["x2_s"] = lambda: final_sent(*x2)
    waits["x2_r"] = lambda: final_came(*x2)

    now("m5_r")
    head_sum = jnp.sum(hd_recv[...].astype(F32), axis=0)
    head_sum = jnp.where(f % 2 == 1, pltpu.roll(head_sum, 64, 1), head_sum)
    ghead_ref[...] = head_sum[0:CLASSES, 0:64]

    now("x2_r")
    two_ref[...] = jnp.sum(x2_recv[...].astype(F32), axis=0).T.reshape(2, 64, 64)
    now("z1_r")
    one_ref[...] = jnp.sum(z1_recv[...].astype(F32), axis=0).T.reshape(2, 64, 64)

    for wait in waits.values():
        wait()


def finish(*refs):
    for i in range(5):
        refs[5 + i][...] = refs[i][...]


def shards(
    node_feats, target_ids, layer_one_nbrs, layer_one_counts, layer_two_nbrs, layer_two_counts, labels,
    layer_one_weight, layer_two_weight, head_weight,
):
    vmem = pl.BlockSpec(memory_space=pltpu.VMEM)
    smem = pl.BlockSpec(memory_space=pltpu.SMEM)
    hbm = pl.BlockSpec(memory_space=pltpu.HBM)
    dma = pltpu.SemaphoreType.DMA
    results = pl.pallas_call(
        kernel,
        out_shape=(
            jax.ShapeDtypeStruct((ROWS, WIDE), BF16),
            jax.ShapeDtypeStruct((SEEDS, CLASSES), F32),
            jax.ShapeDtypeStruct((2, 64, 64), F32),
            jax.ShapeDtypeStruct((2, 64, 64), F32),
            jax.ShapeDtypeStruct((CLASSES, 64), F32),
        ),
        in_specs=[smem, vmem, vmem, hbm, hbm, hbm, vmem, vmem, vmem, vmem],
        out_specs=(hbm, vmem, vmem, vmem, vmem),
        scratch_shapes=[
            pltpu.VMEM((1, FAN1 * TARGETS), jnp.int32),
            pltpu.SMEM((1, FAN1 * TARGETS), jnp.int32),
            pltpu.VMEM((1, TARGETS), F32),
            pltpu.SMEM((1, TARGETS), F32),
            pltpu.VMEM((64, NODES), BF16),
            pltpu.VMEM((NODES + 8, 128), F32),
            pltpu.VMEM((ROWS, 128), F32),
            pltpu.VMEM((16, ROWS, 128), BF16),
            pltpu.VMEM((16, 4, 2, ROWS, 128), BF16),
            pltpu.VMEM((2, 8, 128, 128), BF16),
            pltpu.VMEM((2 * WIDE, WIDE), BF16),
            pltpu.VMEM((128, WIDE), BF16),
            pltpu.VMEM((4, 2, ROWS, 128), F32),
            pltpu.VMEM((4, 2, ROWS, 128), BF16),
            pltpu.VMEM((ROWS, WIDE), BF16),
            pltpu.VMEM((2, 4, SEEDS, 256), BF16),
            pltpu.VMEM((16, SEEDS, 256), BF16),
            pltpu.VMEM((8, SEEDS, 256), BF16),
            pltpu.VMEM((8, 4, 2, SEEDS, 256), BF16),
            pltpu.VMEM((4, 2, 4 * SEEDS, 128), BF16),
            pltpu.VMEM((4, 2, 4 * SEEDS, 128), BF16),
            pltpu.VMEM((4, 2, ROWS, 128), BF16),
            pltpu.VMEM((8, 4, 2, SEEDS, 128), BF16),
            pltpu.VMEM((128, 8 * ROWS), BF16),
            pltpu.VMEM((2, 2, 8, 64, 128), BF16),
            pltpu.VMEM((4, 8, 64, 128), BF16),
            pltpu.VMEM((8, 64, 128), BF16),
            pltpu.VMEM((8, 64, 128), BF16),
            pltpu.VMEM((2, 2, 64, 128), BF16),
            pltpu.VMEM((4, 64, 128), BF16),
            pltpu.VMEM((32, 128), BF16),
            pltpu.VMEM((16, 32, 128), BF16),
            dma((15,)),
            dma((8,)), dma((8,)),
            dma((2,)), dma((2,)),
            dma((16,)), dma((16,)),
            dma((16, 4)), dma((16, 4)),
            dma((16,)), dma((1,)),
            dma((8,)), dma((8,)),
            dma((16,)), dma((16,)),
            dma((8,)), dma((8,)),
            dma((4,)), dma((4,)),
            dma((1,)), dma((1,)),
            dma((8,)), dma((8,)),
            dma((8,)), dma((8,)),
            dma((8, 4)), dma((8, 4)),
            dma((8,)), dma((8,)),
            dma((4,)), dma((4,)),
            dma((16,)), dma((16,)),
        ],
        compiler_params=pltpu.CompilerParams(
            collective_id=0, has_side_effects=True, vmem_limit_bytes=60 * 1024 * 1024
        ),
        name="step",
    )(
        target_ids, layer_one_nbrs.transpose(2, 0, 1), layer_one_counts, node_feats[0].T,
        layer_one_weight.reshape(128, WIDE), layer_two_weight.reshape(2 * WIDE, WIDE), head_weight.T,
        layer_two_nbrs.transpose(2, 0, 1), layer_two_counts, labels,
    )
    hidden, logits, grad_one, grad_two, grad_head = pl.pallas_call(
        finish,
        out_shape=tuple(jax.ShapeDtypeStruct(r.shape, r.dtype) for r in results),
        in_specs=[vmem] * 5,
        out_specs=(vmem,) * 5,
        name="finish",
    )(*results)
    return hidden[None], logits[None], grad_one, grad_two, grad_head.T


def solution(mesh):
    return jax.shard_map(
        shards,
        mesh=mesh,
        in_specs=(
            P("dp", None, "feat"),
            P("dp", None),
            P("dp", None, None),
            P("dp", None),
            P("dp", "feat", None),
            P("dp", "feat"),
            P("dp", "feat"),
            P(None, "feat", None),
            P(),
            P(),
        ),
        out_specs=(
            P("dp", "feat", None),
            P("dp", "feat", None),
            P(None, "feat", "dp"),
            P(None, "feat", "dp"),
            P("feat", None),
        ),
        check_vma=False,
    )
```

```python
import functools

import jax
import jax.numpy as jnp
from jax import lax
from jax.experimental import pallas as pl
from jax.experimental.pallas import tpu as pltpu
from jax.sharding import PartitionSpec as P

MESH = pl.DeviceIdType.MESH
BF16 = jnp.bfloat16
F32 = jnp.float32

NODES = 6144
ROWS = 96
TARGETS = 16 * ROWS
UNROLL = 16
SEEDS = 16
FAN1 = 10
FAN2 = 5
CLASSES = 19
WIDE = 1024
SEQUENCE = (0, 8, 1, 7, 2, 6, 3, 5, 4, 12, 11, 13, 10, 14, 9, 15)
DIRECT = (9, 15)
TRAVEL = {0: 3.0, 1: 6.0, 2: 6.5, 3: 7.5, 4: 8.0}
HOP = 3.0
WX_STEP = 12.0
TN = (((0,), (0,)), ((), ()))
NT = (((1,), (1,)), ((), ()))


def sigmoid(values):
    return 1.0 / (1.0 + jnp.exp(-values))


def silu_slope(values):
    sigma = sigmoid(values)
    return sigma + values * sigma * (1.0 - sigma)


def kernel(
    self_ref, one_nbr_ref, one_cnt_ref, feats_hbm, w1_hbm, w2_hbm, head_ref, nbr_ref, cnt_ref, lab_ref,
    hidden_ref, logits_ref, one_ref, two_ref, ghead_ref,
    idx_vmem, idx_ref, inv_vmem, inv_ref, feats, tab, rows, a_send, a_pool, w1, w2, headp, pre, h_send, hidden_vmem,
    p_send, p_recv, sn_send, sn_pool, b_send, b_pool, g_pool, gu_all, g_turned,
    x1_send, x1_recv, z1_send, z1_recv, x2_send, x2_recv, hd_send, hd_recv,
    load_sem, wa_s, wa_r, wx_s, wx_r, m1_s, m1_r, ma_s, ma_r, ms_s, ms_r, h_s, h_r, m2_s, m2_r,
    sz_s, sz_r, sy_s, sy_r, sc_s, sc_r, m3_s, m3_r, gz_s, gz_r, x1_s, x1_r, z1_s, z1_r, x2_s, x2_r, m5_s, m5_r,
):
    f = lax.axis_index("feat")
    d = lax.axis_index("dp")
    xl, z = f // 8, f % 8
    y, xh, c = d // 4, (d // 2) % 2, d % 2
    x = xh * 2 + xl
    quad = z // 2

    def feat_at(r):
        return ((xl + r // 8) % 2) * 8 + (z + r % 8) % 8

    def feat_from(r):
        return ((xl + r // 8) % 2) * 8 + (z + 8 - r % 8) % 8

    def z_at(r):
        return xl * 8 + (z + r) % 8

    def y_at(r):
        return ((y + r) % 4) * 4 + xh * 2 + c

    def x_at(r):
        to = (x + r) % 4
        return {"feat": (to % 2) * 8 + z, "dp": y * 4 + (to // 2) * 2 + c}

    def yc_at(r):
        return (y + r // 2) % 4, (c + r % 2) % 2

    sibling = y * 4 + xh * 2 + 1 - c

    def send(src, dst, ss, rs, **where):
        return pltpu.make_async_remote_copy(
            src_ref=src, dst_ref=dst, send_sem=ss, recv_sem=rs, device_id=where, device_id_type=MESH
        )

    def loop(lo, hi, fn):
        def body(i, carry):
            fn(i)
            return carry

        lax.fori_loop(lo, hi, body, 0)

    def lanes(block):
        return pl.ds(pl.multiple_of(block * 128, 128), 128)

    waits = {}

    def now(name):
        waits.pop(name)()

    def comm(name, lo, hi, make, start=True):
        if start:
            loop(lo, hi, lambda r: make(r).start())
        waits[name + "_s"] = lambda: loop(lo, hi, lambda r: make(r).wait_send())
        waits[name + "_r"] = lambda: loop(lo, hi, lambda r: make(r).wait_recv())

    barrier = pltpu.get_barrier_semaphore()

    def greet(r):
        pl.semaphore_signal(barrier, inc=1, device_id={"feat": feat_at(r)}, device_id_type=MESH)
        pl.semaphore_signal(barrier, inc=1, device_id={"dp": (d + r) % 16}, device_id_type=MESH)

    loop(1, 16, greet)
    for n in range(1, 4):
        corner = {"feat": (1 - xl) * 8 + z, "dp": y * 4 + ((xh + n // 2) % 2) * 2 + (c + n % 2) % 2}
        pl.semaphore_signal(barrier, inc=1, device_id=corner, device_id_type=MESH)

    w1_load = pltpu.make_async_copy(w1_hbm.at[:, lanes(y * 2 + c)], w1.at[xl, z], load_sem.at[2])
    w1_load.start()
    waits["w1"] = lambda: w1_load.wait()

    def feat_load(i):
        part = pl.ds(pl.multiple_of(i * 1024, 1024), 1024)
        return pltpu.make_async_copy(feats_hbm.at[:, part], feats.at[:, part], load_sem.at[4 + i])

    loop(0, 6, lambda i: feat_load(i).start())
    waits["feats"] = lambda: loop(0, 6, lambda i: feat_load(i).wait())
    w2_load = pltpu.make_async_copy(w2_hbm, w2, load_sem.at[1])
    w2_load.start()
    waits["w2"] = lambda: w2_load.wait()

    one_counts = one_cnt_ref[...]
    for j in range(FAN1):
        idx_vmem[:, j * TARGETS:(j + 1) * TARGETS] = jnp.where(j < one_counts, one_nbr_ref[j], NODES)
    inv_vmem[...] = 1.0 / one_counts.astype(F32)
    idx_load = pltpu.make_async_copy(idx_vmem, idx_ref, load_sem.at[0])
    idx_load.start()
    waits["idx"] = lambda: idx_load.wait()
    inv_load = pltpu.make_async_copy(inv_vmem, inv_ref, load_sem.at[3])
    inv_load.start()
    waits["inv"] = lambda: inv_load.wait()
    headp[...] = jnp.zeros_like(headp)
    headp[0:CLASSES, :] = head_ref[...]

    def wa(r):
        return send(w1.at[xl, z], w1.at[xl, z], wa_s.at[r], wa_r.at[r], feat=z_at(r))

    def wx(n):
        spot = w1.at[xl, pl.ds(xh * 4, 4)]
        return send(spot, spot, wx_s.at[n], wx_r.at[n], **x_at(1 + 2 * n))

    now("w1")
    pl.semaphore_wait(barrier, 33)
    comm("wa", 1, 8, wa)

    waits.pop("feats")

    for i in range(6):
        feat_load(i).wait()
        for first in range(i * 1024, i * 1024 + 1024, 128):
            part = feats[:, first:first + 128]
            tab[first:first + 128, :] = jnp.concatenate([part, part], axis=0).T.astype(F32)
    tab[pl.ds(NODES, 8), :] = jnp.zeros((8, 128), F32)
    now("idx")
    now("inv")

    lane = lax.broadcasted_iota(jnp.int32, (1, 128), 1)
    left = lane < 64

    def gather(k):
        def body(g):
            for u in range(UNROLL):
                local = g * UNROLL + u
                t = k * ROWS + local
                own = tab[pl.ds(self_ref[0, t], 1), :]
                total = [tab[pl.ds(idx_ref[0, j * TARGETS + t], 1), :] for j in range(FAN1)]
                while len(total) > 1:
                    total = [
                        total[i] + total[i + 1] if i + 1 < len(total) else total[i]
                        for i in range(0, len(total), 2)
                    ]
                rows[pl.ds(local, 1), :] = jnp.where(left, own, total[0] * inv_ref[0, t])

        loop(0, ROWS // UNROLL, body)
        a_send[k] = rows[...].astype(BF16)

    def m1(r):
        return send(a_send.at[feat_at(r)], a_pool.at[f, y, c], m1_s.at[r], m1_r.at[r], feat=feat_at(r))

    def ma(r, i):
        spot = a_pool.at[feat_from(r), y, c]
        return send(spot, spot, ma_s.at[r, i], ma_r.at[r, i], dp=y_at(i))

    def ma_two(place, r):
        after = 1 + 2 * (place % 2)
        spot = a_pool.at[feat_from(r), (y + 4 - after) % 4, c]
        return send(spot, spot, ma_s.at[r, 2], ma_r.at[r, 2], dp=y_at(after))

    def ms(r):
        spot = a_pool.at[feat_from(r), :, c]
        return send(spot, spot, ms_s.at[r], ms_r.at[0], dp=sibling)

    def pass_on(place, r):
        if r:
            m1(r).wait_recv()
        for i in (1, 2, 3) if r in DIRECT else (1, 3):
            ma(r, i).start()

    def forward(place, r):
        ma(r, 1 + 2 * (place % 2)).wait_recv()
        ma_two(place, r).start()

    def cross(place, r):
        for i in (1, 2, 3) if r in DIRECT else (2, 3 - 2 * (place % 2)):
            ma(r, i).wait_recv()
        ms(r).start()

    def wx_start(place, r):
        now("wa_r")
        loop(0, 2, lambda n: wx(n).start())

    events = [(WX_STEP, wx_start, 0, 0)]
    for place, r in enumerate(SEQUENCE):
        at = place + 1 + (TRAVEL[min(r % 8, 8 - r % 8)] if r else 0.0)
        events.append((at, pass_on, place, r))
        if r not in DIRECT:
            at += HOP
            events.append((at, forward, place, r))
        events.append((at + HOP, cross, place, r))
    events.sort(key=lambda event: event[0])

    def run_events(until):
        while events and events[0][0] <= until:
            _, act, place, r = events.pop(0)
            act(place, r)

    for place, r in enumerate(SEQUENCE):
        gather(feat_at(r))
        if r:
            m1(r).start()
        else:
            a_pool[f, y, c] = a_send[f]
        run_events(place + 1)
    run_events(1000)
    comm("wx", 0, 2, wx, False)
    waits["m1_s"] = lambda: loop(1, 16, lambda r: m1(r).wait_send())
    waits["ma_s"] = lambda: loop(0, 16, lambda r: loop(1, 4, lambda i: ma(r, i).wait_send()))
    waits["ms_s"] = lambda: loop(0, 16, lambda r: ms(r).wait_send())

    def ms_all():
        send(a_pool.at[:, :, c], a_pool.at[:, :, c], ms_s.at[0], ms_r.at[0], dp=sibling).wait_recv()

    waits["ms_r"] = ms_all
    now("wx_r")
    now("ms_r")

    def hm(r):
        to_y, to_c = yc_at(r)
        return send(
            h_send.at[to_y, to_c], hidden_vmem.at[:, lanes(y * 2 + c)], h_s.at[r], h_r.at[r],
            dp=to_y * 4 + xh * 2 + to_c,
        )

    for q in (2, 1, 3, 0):
        to_y = (y + q) % 4
        wide = jnp.concatenate([a_pool[b, to_y].reshape(2 * ROWS, 128) for b in range(16)], axis=1)
        out = jnp.dot(wide, w1[...].reshape(2048, 128), preferred_element_type=F32)
        pre[to_y] = out.reshape(2, ROWS, 128)
        h_send[to_y] = (out * sigmoid(out)).astype(BF16).reshape(2, ROWS, 128)
        for r in (2 * q, 2 * q + 1):
            if r:
                hm(r).start()
    comm("hm", 1, 8, hm, False)
    hidden_vmem[:, lanes(y * 2 + c)] = h_send[y, c]
    now("hm_r")
    hidden_out = pltpu.make_async_copy(hidden_vmem, hidden_ref, load_sem.at[14])
    hidden_out.start()
    waits["hidden"] = lambda: hidden_out.wait()

    eye = lax.broadcasted_iota(jnp.int32, (SEEDS, SEEDS), 0) == lax.broadcasted_iota(jnp.int32, (SEEDS, SEEDS), 1)

    def column(row):
        return jnp.sum(jnp.where(eye, row, 0), axis=1, keepdims=True)

    counts = column(cnt_ref[...])
    count_float = counts.astype(F32)
    col = lax.broadcasted_iota(jnp.int32, (SEEDS, ROWS), 1)
    table = jnp.zeros((SEEDS, ROWS), F32)
    for j in range(FAN2):
        table = table + jnp.where((column(nbr_ref[j]) == col) & (j < counts), 1.0, 0.0)
    hidden = hidden_vmem[...]
    seed_hidden = hidden[:SEEDS]
    neigh = (jnp.dot(table.astype(BF16), hidden, preferred_element_type=F32) / count_float).astype(BF16)

    wide_left = lax.broadcasted_iota(jnp.int32, (SEEDS, 128), 1) < 64
    for hx in range(2):
        for q in range(4):
            lo = hx * 512 + q * 128
            s = seed_hidden[:, lo:lo + 128].astype(F32)
            n = neigh[:, lo:lo + 128].astype(F32)
            here = slice(hx * 128, hx * 128 + 128)
            sn_send[2 * q, :, here] = jnp.where(wide_left, s, pltpu.roll(n, 64, 1)).astype(BF16)
            sn_send[2 * q + 1, :, here] = jnp.where(wide_left, pltpu.roll(s, 64, 1), n).astype(BF16)

    def sz(r):
        return send(sn_send.at[(z + r) % 8], sn_pool.at[z, y, c], sz_s.at[r], sz_r.at[r], feat=z_at(r))

    comm("sz", 1, 8, sz)
    sn_pool[z, y, c] = sn_send[z]

    now("w2")
    both = jnp.concatenate([seed_hidden, neigh], axis=1)
    upper_pre = jnp.dot(both, w2[...], preferred_element_type=F32)
    upper_sigma = sigmoid(upper_pre)
    upper_hidden = (upper_pre * upper_sigma).astype(BF16)
    logits = lax.dot_general(upper_hidden, headp[...], NT, preferred_element_type=F32)
    logits_ref[...] = logits[:, 0:CLASSES]
    cls = lax.broadcasted_iota(jnp.int32, (SEEDS, 128), 1)
    live = cls < CLASSES
    top = jnp.max(jnp.where(live, logits, -jnp.inf), axis=1, keepdims=True)
    expo = jnp.where(live, jnp.exp(jnp.where(live, logits - top, 0.0)), 0.0)
    probability = expo / jnp.sum(expo, axis=1, keepdims=True)
    one_hot = jnp.where(cls == column(lab_ref[...]), 1.0, 0.0)
    grad_logits = ((probability - one_hot) / 256.0).astype(BF16)

    for hx in range(2):
        for q in range(4):
            lo = hx * 512 + q * 128
            p_send[hx, q, :, 0:128] = upper_hidden[:, lo:lo + 128]
            p_send[hx, q, :, 128:256] = grad_logits

    def m2(r):
        to = feat_at(r)
        return send(p_send.at[to // 8, (to % 8) // 2], p_recv.at[f], m2_s.at[r], m2_r.at[r], feat=to)

    comm("m2", 1, 16, m2)
    p_recv[f] = p_send[xl, quad]

    back_hidden = jnp.dot(grad_logits, headp[...], preferred_element_type=F32)
    slope_two = upper_sigma + upper_pre * upper_sigma * (1.0 - upper_sigma)
    grad_upper = (back_hidden * slope_two).astype(BF16)
    back_two = lax.dot_general(grad_upper, w2[...], NT, preferred_element_type=F32)
    back = jnp.concatenate([back_two[:, 0:WIDE], back_two[:, WIDE:2 * WIDE] / count_float], axis=0)
    back = jnp.concatenate([back.astype(BF16), grad_upper], axis=0)
    wide_table = jnp.concatenate([table, jnp.zeros((SEEDS, 128 - ROWS), F32)], axis=1).astype(BF16)
    for e in range(8):
        b_send[e // 2, e % 2, 0:3 * SEEDS] = back[:, e * 128:e * 128 + 128]
        b_send[e // 2, e % 2, 3 * SEEDS:4 * SEEDS] = wide_table

    def m3(r):
        to_y, to_c = yc_at(r)
        return send(
            b_send.at[to_y, to_c], b_pool.at[y, c], m3_s.at[r], m3_r.at[r], dp=to_y * 4 + xh * 2 + to_c
        )

    comm("m3", 1, 8, m3)
    b_pool[y, c] = b_send[y, c]

    first = jnp.where(lax.broadcasted_iota(jnp.int32, (SEEDS, ROWS), 0) == col, 1.0, 0.0).astype(BF16)
    for r in range(8):
        if r:
            m3(r).wait_recv()
        at_y, at_c = (y + 4 - r // 2) % 4, (c + r) % 2
        terms = b_pool[at_y, at_c]
        spread = jnp.concatenate([first, terms[3 * SEEDS:4 * SEEDS, 0:ROWS]], axis=0)
        rows_back = lax.dot_general(spread, terms[0:2 * SEEDS], TN, preferred_element_type=F32)
        g_pool[at_y, at_c] = (rows_back * silu_slope(pre[at_y, at_c])).astype(BF16)
    waits.pop("m3_r")
    gu_all[z] = b_pool[:, :, 2 * SEEDS:3 * SEEDS]

    def gz(r):
        return send(gu_all.at[z], gu_all.at[z], gz_s.at[r], gz_r.at[r], feat=z_at(r))

    comm("gz", 1, 8, gz)

    g_turned[...] = g_pool[...].reshape(8 * ROWS, 128).T

    def to_final(n, src, dst, ss, rs):
        to_l, to_c = (xl + n // 2) % 2, (c + n % 2) % 2
        return send(src(to_c, to_l), dst(x), ss.at[n], rs.at[x], feat=to_l * 8 + z, dp=y * 4 + c * 2 + to_c)

    def final_start(src, dst, ss, rs):
        pl.when(xh != c)(lambda: to_final(0, src, dst, ss, rs).start())
        loop(1, 4, lambda n: to_final(n, src, dst, ss, rs).start())

        @pl.when(xh == c)
        def _():
            dst(x)[...] = src(c, xl)[...]

    def final_sent(src, dst, ss, rs):
        pl.when(xh != c)(lambda: to_final(0, src, dst, ss, rs).wait_send())
        loop(1, 4, lambda n: to_final(n, src, dst, ss, rs).wait_send())

    def final_came(src, dst, ss, rs):
        def came(n):
            @pl.when(jnp.logical_not((xh == c) & (n == x)))
            def _():
                send(src(0, 0), dst(n), ss.at[1], rs.at[n], feat=f, dp=d).wait_recv()

        loop(0, 4, came)

    def order(i):
        return 4 + (i // 2) * (1 - i % 2) - ((i + 1) // 2) * (i % 2)

    def x1(r):
        to_z = (z + r) % 8
        return (
            lambda to_c, to_l: x1_send.at[to_c, to_l, to_z],
            lambda n: x1_recv.at[n, to_z],
            x1_s.at[r],
            x1_r.at[r],
        )

    for i in range(8):
        to_z = (z + order(i)) % 8
        right = jnp.concatenate(
            [a_pool[to_z].reshape(8 * ROWS, 128), a_pool[8 + to_z].reshape(8 * ROWS, 128)],
            axis=1,
        )
        out = jnp.dot(g_turned[...], right, preferred_element_type=F32).astype(BF16)
        for to_c in range(2):
            for to_l in range(2):
                x1_send[to_c, to_l, to_z] = out[to_c * 64:to_c * 64 + 64, to_l * 128:to_l * 128 + 128]
        final_start(*x1(order(i)))
    waits["x1_s"] = lambda: loop(0, 8, lambda r: final_sent(*x1(r)))

    def sy(r):
        spot = sn_pool.at[:, y, c]
        return send(spot, spot, sy_s.at[r], sy_r.at[r], dp=y_at(r))

    def sc(n):
        spot = sn_pool.at[:, :, c]
        return send(spot, spot, sc_s.at[n], sc_r.at[n], dp=sibling)

    now("sz_r")
    comm("sy", 1, 4, sy)

    def z1(r):
        return send(z1_send.at[r], z1_recv.at[z], z1_s.at[r], z1_r.at[r], feat=z_at(r))

    def z1_start(i):
        r = order(i)
        final_came(*x1(r))
        z1_send[r] = jnp.sum(x1_recv[:, (z + r) % 8].astype(F32), axis=0).astype(BF16)
        pl.when(i < 7)(lambda: z1(r).start())

    loop(0, 8, z1_start)
    comm("z1", 1, 8, z1, False)
    z1_recv[z] = z1_send[0]

    now("sy_r")
    comm("sc", 0, 1, sc)

    now("m2_r")
    every = p_recv[...].reshape(16 * SEEDS, 256)
    head_part = lax.dot_general(every[:, 128:256], every[:, 0:128], TN, preferred_element_type=F32)
    hd_send[...] = head_part[0:32].astype(BF16)

    def m5(r):
        return send(hd_send, hd_recv.at[d], m5_s.at[r], m5_r.at[r], dp=(d + r) % 16)

    comm("m5", 1, 16, m5)
    hd_recv[d] = hd_send[...]

    now("gz_r")
    now("sc_r")
    part_two = lax.dot_general(
        gu_all[...].reshape(64 * SEEDS, 128), sn_pool[...].reshape(64 * SEEDS, 256), TN, preferred_element_type=F32
    ).astype(BF16)
    for to_c in range(2):
        for to_l in range(2):
            x2_send[to_c, to_l] = part_two[to_c * 64:to_c * 64 + 64, to_l * 128:to_l * 128 + 128]

    x2 = (lambda to_c, to_l: x2_send.at[to_c, to_l], lambda n: x2_recv.at[n], x2_s, x2_r)
    final_start(*x2)
    waits["x2_s"] = lambda: final_sent(*x2)
    waits["x2_r"] = lambda: final_came(*x2)

    now("m5_r")
    head_sum = jnp.sum(hd_recv[...].astype(F32), axis=0)
    head_sum = jnp.where(f % 2 == 1, pltpu.roll(head_sum, 64, 1), head_sum)
    ghead_ref[...] = head_sum[0:CLASSES, 0:64]

    now("x2_r")
    two_ref[...] = jnp.sum(x2_recv[...].astype(F32), axis=0).T.reshape(2, 64, 64)
    now("z1_r")
    one_ref[...] = jnp.sum(z1_recv[...].astype(F32), axis=0).T.reshape(2, 64, 64)

    for wait in waits.values():
        wait()


def finish(*refs):
    for i in range(5):
        refs[5 + i][...] = refs[i][...]


def shards(
    node_feats, target_ids, layer_one_nbrs, layer_one_counts, layer_two_nbrs, layer_two_counts, labels,
    layer_one_weight, layer_two_weight, head_weight,
):
    vmem = pl.BlockSpec(memory_space=pltpu.VMEM)
    smem = pl.BlockSpec(memory_space=pltpu.SMEM)
    hbm = pl.BlockSpec(memory_space=pltpu.HBM)
    dma = pltpu.SemaphoreType.DMA
    results = pl.pallas_call(
        kernel,
        out_shape=(
            jax.ShapeDtypeStruct((ROWS, WIDE), BF16),
            jax.ShapeDtypeStruct((SEEDS, CLASSES), F32),
            jax.ShapeDtypeStruct((2, 64, 64), F32),
            jax.ShapeDtypeStruct((2, 64, 64), F32),
            jax.ShapeDtypeStruct((CLASSES, 64), F32),
        ),
        in_specs=[smem, vmem, vmem, hbm, hbm, hbm, vmem, vmem, vmem, vmem],
        out_specs=(hbm, vmem, vmem, vmem, vmem),
        scratch_shapes=[
            pltpu.VMEM((1, FAN1 * TARGETS), jnp.int32),
            pltpu.SMEM((1, FAN1 * TARGETS), jnp.int32),
            pltpu.VMEM((1, TARGETS), F32),
            pltpu.SMEM((1, TARGETS), F32),
            pltpu.VMEM((64, NODES), BF16),
            pltpu.VMEM((NODES + 8, 128), F32),
            pltpu.VMEM((ROWS, 128), F32),
            pltpu.VMEM((16, ROWS, 128), BF16),
            pltpu.VMEM((16, 4, 2, ROWS, 128), BF16),
            pltpu.VMEM((2, 8, 128, 128), BF16),
            pltpu.VMEM((2 * WIDE, WIDE), BF16),
            pltpu.VMEM((128, WIDE), BF16),
            pltpu.VMEM((4, 2, ROWS, 128), F32),
            pltpu.VMEM((4, 2, ROWS, 128), BF16),
            pltpu.VMEM((ROWS, WIDE), BF16),
            pltpu.VMEM((2, 4, SEEDS, 256), BF16),
            pltpu.VMEM((16, SEEDS, 256), BF16),
            pltpu.VMEM((8, SEEDS, 256), BF16),
            pltpu.VMEM((8, 4, 2, SEEDS, 256), BF16),
            pltpu.VMEM((4, 2, 4 * SEEDS, 128), BF16),
            pltpu.VMEM((4, 2, 4 * SEEDS, 128), BF16),
            pltpu.VMEM((4, 2, ROWS, 128), BF16),
            pltpu.VMEM((8, 4, 2, SEEDS, 128), BF16),
            pltpu.VMEM((128, 8 * ROWS), BF16),
            pltpu.VMEM((2, 2, 8, 64, 128), BF16),
            pltpu.VMEM((4, 8, 64, 128), BF16),
            pltpu.VMEM((8, 64, 128), BF16),
            pltpu.VMEM((8, 64, 128), BF16),
            pltpu.VMEM((2, 2, 64, 128), BF16),
            pltpu.VMEM((4, 64, 128), BF16),
            pltpu.VMEM((32, 128), BF16),
            pltpu.VMEM((16, 32, 128), BF16),
            dma((15,)),
            dma((8,)), dma((8,)),
            dma((2,)), dma((2,)),
            dma((16,)), dma((16,)),
            dma((16, 4)), dma((16, 4)),
            dma((16,)), dma((1,)),
            dma((8,)), dma((8,)),
            dma((16,)), dma((16,)),
            dma((8,)), dma((8,)),
            dma((4,)), dma((4,)),
            dma((1,)), dma((1,)),
            dma((8,)), dma((8,)),
            dma((8,)), dma((8,)),
            dma((8, 4)), dma((8, 4)),
            dma((8,)), dma((8,)),
            dma((4,)), dma((4,)),
            dma((16,)), dma((16,)),
        ],
        compiler_params=pltpu.CompilerParams(
            collective_id=0, has_side_effects=True, vmem_limit_bytes=60 * 1024 * 1024
        ),
        name="step",
    )(
        target_ids, layer_one_nbrs.transpose(2, 0, 1), layer_one_counts, node_feats[0].T,
        layer_one_weight.reshape(128, WIDE), layer_two_weight.reshape(2 * WIDE, WIDE), head_weight.T,
        layer_two_nbrs.transpose(2, 0, 1), layer_two_counts, labels,
    )
    hidden, logits, grad_one, grad_two, grad_head = pl.pallas_call(
        finish,
        out_shape=tuple(jax.ShapeDtypeStruct(r.shape, r.dtype) for r in results),
        in_specs=[vmem] * 5,
        out_specs=(vmem,) * 5,
        name="finish",
    )(*results)
    return hidden[None], logits[None], grad_one, grad_two, grad_head.T


def solution(mesh):
    return jax.shard_map(
        shards,
        mesh=mesh,
        in_specs=(
            P("dp", None, "feat"),
            P("dp", None),
            P("dp", None, None),
            P("dp", None),
            P("dp", "feat", None),
            P("dp", "feat"),
            P("dp", "feat"),
            P(None, "feat", None),
            P(),
            P(),
        ),
        out_specs=(
            P("dp", "feat", None),
            P("dp", "feat", None),
            P(None, "feat", "dp"),
            P(None, "feat", "dp"),
            P("feat", None),
        ),
        check_vma=False,
    )
```
